32 devices in a mesh: mem: 8 (over z, x), gx: 2 (over core), gy: 2 (over y).
Axes of the slice: x: 2, y: 2, z: 4, core: 2. Of those that a mesh axis runs over, the one named last changes fastest.
Arguments:
- fields: float32 [32, 3, 256, 256], P('mem', None, 'gx', 'gy'), may hold values from -3 to 3
- noise: float32 [16, 256, 256], P('mem', 'gx', 'gy'), may hold values from -6 to 6
- ancestors: int32 [2, 2, 16], P('gx', 'gy'), may hold values from 0 to 15
- obs_cells: int32 [2, 2, 256], P('gx', 'gy'), may hold values from 0 to 16383
- obs_values: float32 [2, 2, 256], P('gx', 'gy'), may hold values from -3 to 12
Outputs:
- resampled: float32 [32, 3, 256, 256], P('mem', None, 'gx', 'gy')
- log_weights: float32 [2, 2, 32], P('gx', 'gy', 'mem')
The draws below stay inside these ranges and needn't reach their ends.
All inputs are finite; a program needn't handle non-finite values.
Results may differ from the reference program's by a relative error of at most 0.00012.
Values sent between devices are 32-bit elements; how exact they have to be, the bound alone decides.
A program may use at most 128 MiB of HBM per device.

```python
import math
import jax
import jax.numpy as jnp
import numpy as np

CX = 128
CY = 128
OBS = 256
MEMBERS = 32
PAIRS = 16
NX = 256
NY = 256
N_GX = 2
N_GY = 2


def draw_fields(key, part):
    key_vals = jax.random.fold_in(key, 21)
    key_order = jax.random.fold_in(key, 22)
    tiles = N_GX * N_GY
    base = jax.random.normal(key_vals, (MEMBERS, 3, NX, NY), jnp.float32)
    table = jnp.array([0.25, 0.5, 0.8, 1.2], jnp.float32)
    order = jax.random.permutation(key_order, jnp.arange(tiles, dtype=jnp.int32) % 4)
    tile_scale = jnp.take(table, order).reshape(N_GX, N_GY)
    cell_scale = jnp.repeat(jnp.repeat(tile_scale, CX, axis=0), CY, axis=1)
    return jnp.clip(base * cell_scale[None, None, :, :], -3.0, 3.0).astype(jnp.float32)


def draw_obs_values(key, part):
    key_base = jax.random.fold_in(key, 11)
    key_order = jax.random.fold_in(key, 12)
    tiles = N_GX * N_GY
    base = jnp.clip(0.3 * jax.random.normal(key_base, (N_GX, N_GY, OBS), jnp.float32), -1.2, 1.2)
    table = jnp.array([0.0, 300.0, 600.0, 1200.0], jnp.float32)
    order = jax.random.permutation(key_order, jnp.arange(tiles, dtype=jnp.int32) % 4)
    strength = jnp.take(table, order).reshape(N_GX, N_GY, 1)
    offset = jnp.sqrt(strength / (2.0 * OBS))
    return (base + offset).astype(jnp.float32)


def plant(values, stream_key, low, top_value):
    longest = values.shape.index(max(values.shape))
    spots = []
    for shift in (0, 1):
        where = [jax.random.randint(jax.random.fold_in(stream_key, axis), (), 0, length) for axis, length in enumerate(values.shape)]
        where[longest] = (where[longest] + shift) % values.shape[longest]
        spots.append(tuple(where))
    return values.at[spots[0]].set(low).at[spots[1]].set(top_value)


def steps_of(stream_key, dims, cuts, low, top_value):
    factor_of = 1.0
    for dim, parts in cuts:
        draws = jax.random.uniform(jax.random.fold_in(jax.random.fold_in(stream_key, 6), dim), (parts,), jnp.float32, low / len(cuts), top_value / len(cuts))
        factor_of = factor_of * jnp.repeat(jnp.exp(draws), dims[dim] // parts).reshape((-1,) + (1,) * (len(dims) - 1 - dim))
    return factor_of


def rank_bounds(count, slope):
    weights = [(1 << 20) // math.isqrt(standing ** slope) + 1 for standing in range(1, count + 1)]
    scale = 1 + sum(weights) // (1 << 30)
    return np.cumsum(np.array([max(1, weight // scale) for weight in weights]))


def ranked_ids(rng, shape, count, skew):
    table = rank_bounds(count, skew)
    lot = jax.random.randint(jax.random.fold_in(rng, 1), shape, 0, int(table[count - 1]))
    standing = jnp.searchsorted(jnp.asarray(table, jnp.int32), lot, side="right")
    return jax.random.permutation(jax.random.fold_in(rng, 2), count)[standing].astype(jnp.int32)


def gaussian(stream_key, dims, width, limit, split=(), held_as=jnp.bfloat16):
    drawn = jax.random.normal(stream_key, dims, jnp.float32) * width
    if len(split) > 0:
        drawn = steps_of(stream_key, dims, split, -0.22, 0.18) * drawn
    return jnp.clip(drawn, min=-limit, max=limit).astype(held_as)


def setup_inputs(seed: int = 0) -> dict:
    keys = jax.random.split(jax.random.key(seed), 6)
    return {
        "fields": draw_fields(jax.random.fold_in(keys[5], 71), 0),
        "noise": gaussian(keys[1], (PAIRS, NX, NY), 1.0, 6.0, ((0, 8), (1, 2), (2, 2)), jnp.float32),
        "ancestors": plant(ranked_ids(keys[2], (N_GX, N_GY, PAIRS), PAIRS, 2), jax.random.fold_in(keys[2], 3), 0, PAIRS - 1).astype(jnp.int32),
        "obs_cells": plant(jax.random.randint(keys[3], (N_GX, N_GY, OBS), 0, CX * CY), jax.random.fold_in(keys[3], 1), 0, (CX * CY) - 1).astype(jnp.int32),
        "obs_values": draw_obs_values(jax.random.fold_in(keys[5], 71), 0),
    }


COURANT = 0.3
DIFFUSE = 0.05
HYPER = 0.005
NOISE_AMP = 0.1
OBS_VAR = 0.25


def xdiff(a):
    return (jnp.roll(a, -1, -2) - jnp.roll(a, 1, -2)) * 0.5


def ydiff(a):
    return (jnp.roll(a, -1, -1) - jnp.roll(a, 1, -1)) * 0.5


def laplace(a):
    return jnp.roll(a, -1, -2) + jnp.roll(a, 1, -2) + jnp.roll(a, -1, -1) + jnp.roll(a, 1, -1) - 4.0 * a


def smooth(a):
    return DIFFUSE * laplace(a) - HYPER * laplace(laplace(a))


def advance(eta, speed_x, speed_y, force, coriolis):
    depth = 1.0 + eta
    tend_h = xdiff(depth * speed_x) + ydiff(depth * speed_y)
    tend_u = speed_x * xdiff(speed_x) + speed_y * ydiff(speed_x) + xdiff(eta) - coriolis * speed_y
    tend_v = speed_x * xdiff(speed_y) + speed_y * ydiff(speed_y) + ydiff(eta) + coriolis * speed_x
    new_eta = eta - COURANT * tend_h + smooth(eta) + NOISE_AMP * force
    new_u = speed_x - COURANT * tend_u + smooth(speed_x)
    new_v = speed_y - COURANT * tend_v + smooth(speed_y)
    return new_eta, new_u, new_v


def reference(fields, noise, ancestors, obs_cells, obs_values):
    rows_y = jnp.arange(NY, dtype=jnp.int32).astype(jnp.float32)
    coriolis = 0.1 + 0.2 * ((rows_y + 0.5) / NY - 0.5)
    force = jnp.repeat(noise, 2, axis=0)
    eta, speed_x, speed_y = fields[:, 0], fields[:, 1], fields[:, 2]
    for step in range(2):
        eta, speed_x, speed_y = advance(eta, speed_x, speed_y, force, coriolis)
    state = jnp.stack([eta, speed_x, speed_y], axis=1)
    tiles = eta.reshape(MEMBERS, N_GX, CX, N_GY, CY).transpose(1, 3, 0, 2, 4).reshape(N_GX, N_GY, MEMBERS, CX * CY)
    values = jnp.take_along_axis(tiles, obs_cells[:, :, None, :].astype(jnp.int32), axis=3)
    misfit = values - obs_values[:, :, None, :]
    logw = -0.5 * jnp.sum(misfit * misfit, axis=3) / OBS_VAR
    peak = jnp.max(logw, axis=2, keepdims=True)
    expo = jnp.exp(logw - peak)
    log_weights = logw - peak - jnp.log(jnp.sum(expo, axis=2, keepdims=True))
    blocks = state.reshape(MEMBERS, 3, N_GX, CX, N_GY, CY).transpose(2, 4, 0, 1, 3, 5)
    slots = jnp.arange(MEMBERS, dtype=jnp.int32)
    source = 2 * jnp.take(ancestors, slots // 2, axis=2) + slots % 2
    picked = jnp.take_along_axis(blocks, source[:, :, :, None, None, None].astype(jnp.int32), axis=2)
    resampled = picked.transpose(2, 3, 0, 4, 1, 5).reshape(MEMBERS, 3, NX, NY)
    return resampled, log_weights
```

```python
import functools

import jax
import jax.numpy as jnp
from jax import lax
from jax.experimental import pallas as pl
from jax.experimental.pallas import tpu as pltpu
from jax.sharding import PartitionSpec as P

COURANT = 0.3
NOISE_AMP = 0.1
MESH = pl.DeviceIdType.MESH
BASE = 16
EDGE = 8
STRIPE = 32
CHUNK = 16


def roll_y(a, shift):
    return pltpu.roll(a, shift % a.shape[-1], 1)


def advance(get, force, coriolis):
    def parts(comp):
        mid, low, high = get(comp, 0), get(comp, -1), get(comp, 1)
        near = low + high
        far = get(comp, -2) + get(comp, 2)
        left, right = roll_y(mid, 1), roll_y(mid, -1)
        cross = 0.09 * mid - 0.01 * near
        smooth = (
            0.7 * mid
            + 0.09 * near
            - 0.005 * far
            + roll_y(cross - 0.005 * right, -1)
            + roll_y(cross - 0.005 * left, 1)
        )
        return mid, low, high, left, right, smooth

    _, eta_lo, eta_hi, eta_le, eta_ri, eta_s = parts(0)
    u, u_lo, u_hi, u_le, u_ri, u_s = parts(1)
    v, v_lo, v_hi, v_le, v_ri, v_s = parts(2)
    flux = (
        (1.0 + eta_hi) * u_hi
        - (1.0 + eta_lo) * u_lo
        + (1.0 + eta_ri) * v_ri
        - (1.0 + eta_le) * v_le
    )
    half = 0.5 * COURANT
    new_eta = eta_s - half * flux + NOISE_AMP * force
    turn = COURANT * coriolis
    new_u = u_s - half * (u * (u_hi - u_lo) + v * (u_ri - u_le) + (eta_hi - eta_lo)) + turn * v
    new_v = v_s - half * (u * (v_hi - v_lo) + v * (v_ri - v_le) + (eta_ri - eta_le)) - turn * u
    return new_eta, new_u, new_v


def kernel(
    cfg,
    fields_ref,
    noise_ref,
    anc_ref,
    cells_ref,
    values_ref,
    out_ref,
    weights_ref,
    old,
    mid,
    force,
    seam_own,
    seam_old,
    seam_mid,
    seam_new,
    pack_out,
    pack_in,
    logw_out,
    logw_all,
    *rest,
):
    n, inner, outer, members, count_x, count_y = cfg
    pairs = members // 2
    parts = 6
    gathered = rest[0:parts]
    offered = rest[parts : 2 * parts]
    taken = rest[2 * parts : 3 * parts]
    (rim_send, rim_recv, w_send, w_recv, z_send, z_recv, x_send, x_recv) = rest[3 * parts :]

    mem, gx, gy = lax.axis_index("mem"), lax.axis_index("gx"), lax.axis_index("gy")
    place, line = lax.rem(mem, inner), lax.div(mem, inner)
    near_x, near_y, diagonal = (mem, 1 - gx, gy), (mem, gx, 1 - gy), (mem, 1 - gx, 1 - gy)

    barrier = pltpu.get_barrier_semaphore()
    for peer in (near_x, near_y, diagonal):
        pl.semaphore_signal(barrier, inc=1, device_id=peer, device_id_type=MESH)
    for d in range(1, n):
        pl.semaphore_signal(
            barrier, inc=1, device_id=(lax.rem(mem + d, n), gx, gy), device_id_type=MESH
        )

    lane = lax.broadcasted_iota(jnp.int32, (1, count_y), 1)
    spot = lane & (STRIPE - 1)
    owner = lane >> 5
    group = spot >> 2
    packed_comp = jnp.where((group & 1) == 1, group >> 1, ((group >> 1) + 1) & 3)

    def seam_of(rows, size, comp):
        total = jnp.zeros((size, count_y), jnp.float32)
        for m in range(members):
            plane = force[m // 2, rows, :] if comp == 3 else old[m, comp, rows, :]
            low = roll_y(plane, 8 + STRIPE * m)
            high = roll_y(plane, 24 + STRIPE * m)
            total = jnp.where(owner == m, jnp.where(spot < 16, low, high), total)
        return total

    def load(i, carry):
        rows = pl.ds(pl.multiple_of(i * CHUNK, CHUNK), CHUNK)
        padded = pl.ds(pl.multiple_of(i * CHUNK + BASE, CHUNK), CHUNK)
        for m in range(members):
            for comp in range(3):
                old[m, comp, padded, :] = fields_ref[m, comp, rows, :]
        for p in range(pairs):
            force[p, padded, :] = noise_ref[p, rows, :]
        packed = jnp.zeros((CHUNK, count_y), jnp.float32)
        for comp in range(4):
            seam = seam_of(padded, CHUNK, comp)
            seam_own[comp, padded, :] = seam
            packed = jnp.where(packed_comp == comp, roll_y(seam, 8 * comp), packed)
        pack_out[rows, :] = packed
        return carry

    lax.fori_loop(0, count_x // CHUNK, load, 0)
    pl.semaphore_wait(barrier, n + 2)

    top = BASE + count_x
    first, last = pl.ds(0, EDGE), pl.ds(count_x - EDGE, EDGE)
    rim_low, rim_high = pl.ds(BASE - EDGE, EDGE), pl.ds(top, EDGE)
    moves = [
        (pack_out, pack_in.at[pl.ds(BASE, count_x), :], near_y),
        (fields_ref.at[:, :, last, :], old.at[:, :, rim_low, :], near_x),
        (fields_ref.at[:, :, first, :], old.at[:, :, rim_high, :], near_x),
        (noise_ref.at[:, last, :], force.at[:, rim_low, :], near_x),
        (noise_ref.at[:, first, :], force.at[:, rim_high, :], near_x),
        (pack_out.at[last, :], pack_in.at[rim_low, :], diagonal),
        (pack_out.at[first, :], pack_in.at[rim_high, :], diagonal),
    ]
    rims = []
    for k, (src, dst, peer) in enumerate(moves):
        rims.append(
            pltpu.make_async_remote_copy(
                src_ref=src,
                dst_ref=dst,
                send_sem=rim_send.at[k],
                recv_sem=rim_recv.at[k],
                device_id=peer,
                device_id_type=MESH,
            )
        )
    for copy in rims:
        copy.start()
    for copy in rims[1:5]:
        copy.wait_recv()

    total_y = 2 * count_y

    def turning(local):
        rows_y = lax.rem(gy * count_y + local + total_y, total_y)
        return 0.1 + 0.2 * ((rows_y.astype(jnp.float32) + 0.5) / total_y - 0.5)

    cor_tile = turning(lane)
    cor_seam = turning(jnp.where(spot < 16, spot - 8, spot - 24 + count_y))

    wide = (count_x + 2 * EDGE) // CHUNK

    def first_step(i, carry):
        m, at = lax.div(i, wide), pl.multiple_of(lax.rem(i, wide) * CHUNK + EDGE, EDGE)
        new = advance(
            lambda comp, d: old[m, comp, pl.ds(at + d, CHUNK), :],
            force[lax.div(m, 2), pl.ds(at, CHUNK), :],
            cor_tile,
        )
        for comp in range(3):
            mid[m, comp, pl.ds(at, CHUNK), :] = new[comp]
        return carry

    lax.fori_loop(0, members * wide, first_step, 0)

    for start in (BASE - EDGE, top):
        rows = pl.ds(start, EDGE)
        for comp in range(4):
            seam_own[comp, rows, :] = seam_of(rows, EDGE, comp)
    for copy in (rims[0], rims[5], rims[6]):
        copy.wait_recv()

    def seam_fill(i, carry):
        rows = pl.ds(pl.multiple_of(i * CHUNK + EDGE, EDGE), CHUNK)
        packed = pack_in[rows, :]
        for comp in range(4):
            seam_old[comp, rows, :] = jnp.where(
                (spot >= 8) & (spot < 24), seam_own[comp, rows, :], roll_y(packed, -8 * comp)
            )
        return carry

    lax.fori_loop(0, wide, seam_fill, 0)

    def seam_step(source, target):
        def body(i, carry):
            at = pl.multiple_of(i * CHUNK + EDGE, EDGE)
            new = advance(
                lambda comp, d: source[comp, pl.ds(at + d, CHUNK), :],
                seam_old[3, pl.ds(at, CHUNK), :],
                cor_seam,
            )
            for comp in range(3):
                target[comp, pl.ds(at, CHUNK), :] = new[comp]
            return carry

        lax.fori_loop(0, wide, body, 0)

    seam_step(seam_old, seam_mid)
    seam_step(seam_mid, seam_new)

    def z_copy(part, origin, right):
        way = 0 if right else 1
        peer = line + 1 if right else line - 1
        block = gathered[part].at[origin]
        return pltpu.make_async_remote_copy(
            src_ref=block,
            dst_ref=block,
            send_sem=z_send.at[way, part, origin],
            recv_sem=z_recv.at[way, part, origin],
            device_id=(peer * inner + place, gx, gy),
            device_id_type=MESH,
        )

    for e in range(2):
        for p in range(pairs):
            m = 2 * p + e

            def second_step(i, carry, m=m, p=p, e=e):
                row = pl.multiple_of(i * CHUNK, CHUNK)
                at = row + BASE
                new = advance(
                    lambda comp, d: mid[m, comp, pl.ds(at + d, CHUNK), :],
                    force[p, pl.ds(at, CHUNK), :],
                    cor_tile,
                )
                for comp in range(3):
                    seam = seam_new[comp, pl.ds(at, CHUNK), :]
                    low, high = roll_y(seam, -(STRIPE * m + 8)), roll_y(seam, -(STRIPE * m + 24))
                    whole = jnp.where(lane < 4, low, jnp.where(lane >= count_y - 4, high, new[comp]))
                    gathered[3 * e + comp][line, p, pl.ds(row, CHUNK), :] = whole
                return carry

            lax.fori_loop(0, count_x // CHUNK, second_step, 0)
        for comp in range(3):
            part = 3 * e + comp

            @pl.when(line < outer - 1)
            def _(part=part):
                z_copy(part, line, True).start()

            @pl.when(line > 0)
            def _(part=part):
                z_copy(part, line, False).start()

    cells = cells_ref[...]
    hot_y = jnp.where(
        lax.broadcasted_iota(jnp.int32, (count_y, cells.shape[1]), 0) == lax.rem(cells, count_y),
        1.0,
        0.0,
    )
    hot_x = lax.broadcasted_iota(jnp.int32, (count_x, cells.shape[1]), 0) == lax.div(cells, count_y)
    tile_lane = lax.broadcasted_iota(jnp.int32, (8, 128), 1)
    own = jnp.zeros((8, 128), jnp.float32)
    for m in range(members):
        picked = jnp.dot(
            gathered[3 * (m % 2)][line, m // 2],
            hot_y,
            precision=lax.Precision.HIGHEST,
            preferred_element_type=jnp.float32,
        )
        seen = jnp.sum(jnp.where(hot_x, picked, 0.0), axis=0, keepdims=True)
        misfit = seen - values_ref[...]
        logw = -2.0 * jnp.sum(misfit * misfit, axis=1, keepdims=True)
        own = jnp.where(tile_lane == m, logw, own)
    logw_out[...] = own
    logw_all[mem] = own

    def w_copy(d):
        return pltpu.make_async_remote_copy(
            src_ref=logw_out,
            dst_ref=logw_all.at[mem],
            send_sem=w_send.at[d],
            recv_sem=w_recv.at[d],
            device_id=(lax.rem(mem + d, n), gx, gy),
            device_id_type=MESH,
        )

    for d in range(1, n):
        w_copy(d).start()

    def x_copy(part, d):
        return pltpu.make_async_remote_copy(
            src_ref=offered[part].at[d],
            dst_ref=taken[part].at[place],
            send_sem=x_send.at[part, d],
            recv_sem=x_recv.at[part, d],
            device_id=(line * inner + lax.rem(place + d, inner), gx, gy),
            device_id_type=MESH,
        )

    def finish(part):
        e, comp = part // 3, part % 3
        for d in range(1, inner):
            x_copy(part, d).wait_recv()
        for s in range(pairs):
            source = lax.rem(lax.div(anc_ref[0, mem * pairs + s], pairs), inner)
            out_ref[2 * s + e, comp] = taken[part][source, s]

    for part in range(parts):
        for t in range(1, outer):

            @pl.when(line - t >= 0)
            def _(part=part, t=t):
                z_copy(part, line - t, True).wait_recv()

                @pl.when(line < outer - 1)
                def _():
                    z_copy(part, line - t, True).start()

            @pl.when(line + t < outer)
            def _(part=part, t=t):
                z_copy(part, line + t, False).wait_recv()

                @pl.when(line > 0)
                def _():
                    z_copy(part, line + t, False).start()

        for d in range(inner):
            goal = line * inner + lax.rem(place + d, inner)
            for s in range(pairs):
                wanted = anc_ref[0, goal * pairs + s]
                origin = lax.div(lax.div(wanted, pairs), inner)
                block = gathered[part][origin, lax.rem(wanted, pairs)]
                if d == 0:
                    taken[part][place, s] = block
                else:
                    offered[part][d, s] = block
            if d > 0:
                x_copy(part, d).start()
        if part > 0:
            finish(part - 1)
    finish(parts - 1)

    for d in range(1, n):
        w_copy(d).wait_recv()
    every = logw_all[...]
    real = lax.broadcasted_iota(jnp.int32, every.shape, 2) < members
    once = lax.broadcasted_iota(jnp.int32, every.shape, 1) == 0
    every_max = jnp.max(jnp.where(real, every, -jnp.inf), axis=0)
    peak = jnp.max(every_max, axis=1, keepdims=True)
    expo = jnp.where(real & once, jnp.exp(jnp.where(real, every - peak[None], 0.0)), 0.0)
    total = jnp.sum(jnp.sum(jnp.sum(expo, axis=0), axis=1, keepdims=True), axis=0, keepdims=True)
    normal = own - peak - jnp.log(total)
    weights_ref[...] = normal[0:1, 0:members]

    for copy in rims:
        copy.wait_send()
    for d in range(1, n):
        w_copy(d).wait_send()
    for part in range(parts):
        for d in range(1, inner):
            x_copy(part, d).wait_send()
        for t in range(outer):

            @pl.when((line - t >= 0) & (line < outer - 1))
            def _(part=part, t=t):
                z_copy(part, line - t, True).wait_send()

            @pl.when((line + t < outer) & (line > 0))
            def _(part=part, t=t):
                z_copy(part, line + t, False).wait_send()


def shards(n, fields, noise, ancestors, obs_cells, obs_values):
    members, comps, count_x, count_y = fields.shape
    inner = 1
    while inner * inner * 4 <= n:
        inner *= 2
    outer = n // inner
    pairs = members // 2
    rows = count_x + 2 * BASE
    f32 = jnp.float32
    vmem = pl.BlockSpec(memory_space=pltpu.VMEM)
    dma = pltpu.SemaphoreType.DMA
    parts = 2 * comps
    plane = (count_x, count_y)
    scratch = [
        pltpu.VMEM((members, 3, rows, count_y), f32),
        pltpu.VMEM((members, 3, rows, count_y), f32),
        pltpu.VMEM((pairs, rows, count_y), f32),
        pltpu.VMEM((4, rows, count_y), f32),
        pltpu.VMEM((4, rows, count_y), f32),
        pltpu.VMEM((3, rows, count_y), f32),
        pltpu.VMEM((3, rows, count_y), f32),
        pltpu.VMEM(plane, f32),
        pltpu.VMEM((rows, count_y), f32),
        pltpu.VMEM((8, 128), f32),
        pltpu.VMEM((n, 8, 128), f32),
    ]
    scratch += [pltpu.VMEM((outer, pairs) + plane, f32)] * parts
    scratch += [pltpu.VMEM((inner, pairs) + plane, f32)] * (2 * parts)
    scratch += [
        dma((7,)),
        dma((7,)),
        dma((n,)),
        dma((n,)),
        dma((2, parts, outer)),
        dma((2, parts, outer)),
        dma((parts, inner)),
        dma((parts, inner)),
    ]
    resampled, weights = pl.pallas_call(
        functools.partial(kernel, (n, inner, outer, members, count_x, count_y)),
        out_shape=(
            jax.ShapeDtypeStruct(fields.shape, f32),
            jax.ShapeDtypeStruct((1, members), f32),
        ),
        in_specs=[vmem, vmem, pl.BlockSpec(memory_space=pltpu.SMEM), vmem, vmem],
        out_specs=(vmem, vmem),
        scratch_shapes=scratch,
        compiler_params=pltpu.CompilerParams(
            collective_id=0, has_side_effects=True, vmem_limit_bytes=48 * 1024 * 1024
        ),
    )(
        fields,
        noise,
        ancestors.reshape(1, -1),
        obs_cells.reshape(1, -1),
        obs_values.reshape(1, -1),
    )
    return resampled, weights.reshape(1, 1, members)


def solution(mesh):
    return jax.shard_map(
        functools.partial(shards, mesh.shape["mem"]),
        mesh=mesh,
        in_specs=(
            P("mem", None, "gx", "gy"),
            P("mem", "gx", "gy"),
            P("gx", "gy", None),
            P("gx", "gy", None),
            P("gx", "gy", None),
        ),
        out_specs=(P("mem", None, "gx", "gy"), P("gx", "gy", "mem")),
        check_vma=False,
    )
```

```python
import functools

import jax
import jax.numpy as jnp
from jax import lax
from jax.experimental import pallas as pl
from jax.experimental.pallas import tpu as pltpu
from jax.sharding import PartitionSpec as P

COURANT = 0.3
NOISE_AMP = 0.1
MESH = pl.DeviceIdType.MESH
BASE = 16
EDGE = 8
STRIPE = 32
CHUNK = 16


def roll_y(a, shift):
    return pltpu.roll(a, shift % a.shape[-1], 1)


def advance(get, force, coriolis):
    def parts(comp):
        mid, low, high = get(comp, 0), get(comp, -1), get(comp, 1)
        near = low + high
        far = get(comp, -2) + get(comp, 2)
        left, right = roll_y(mid, 1), roll_y(mid, -1)
        cross = 0.09 * mid - 0.01 * near
        smooth = (
            0.7 * mid
            + 0.09 * near
            - 0.005 * far
            + roll_y(cross - 0.005 * right, -1)
            + roll_y(cross - 0.005 * left, 1)
        )
        return mid, low, high, left, right, smooth

    _, eta_lo, eta_hi, eta_le, eta_ri, eta_s = parts(0)
    u, u_lo, u_hi, u_le, u_ri, u_s = parts(1)
    v, v_lo, v_hi, v_le, v_ri, v_s = parts(2)
    flux = (
        (1.0 + eta_hi) * u_hi
        - (1.0 + eta_lo) * u_lo
        + (1.0 + eta_ri) * v_ri
        - (1.0 + eta_le) * v_le
    )
    half = 0.5 * COURANT
    new_eta = eta_s - half * flux + NOISE_AMP * force
    turn = COURANT * coriolis
    new_u = u_s - half * (u * (u_hi - u_lo) + v * (u_ri - u_le) + (eta_hi - eta_lo)) + turn * v
    new_v = v_s - half * (u * (v_hi - v_lo) + v * (v_ri - v_le) + (eta_ri - eta_le)) - turn * u
    return new_eta, new_u, new_v


def kernel(
    cfg,
    fields_ref,
    noise_ref,
    anc_ref,
    cells_ref,
    values_ref,
    out_ref,
    weights_ref,
    old,
    mid,
    force,
    seam_own,
    seam_old,
    seam_mid,
    seam_new,
    pack_out,
    pack_in,
    logw_out,
    logw_all,
    *rest,
):
    n, inner, outer, members, count_x, count_y = cfg
    pairs = members // 2
    parts = 6
    gathered = rest[0:parts]
    offered = rest[parts : 2 * parts]
    taken = rest[2 * parts : 3 * parts]
    end_out = rest[3 * parts : 4 * parts]
    end_in = rest[4 * parts : 5 * parts]
    (rim_send, rim_recv, w_send, w_recv, z_send, z_recv) = rest[5 * parts : 5 * parts + 6]
    (x_send, x_recv, end_send, end_recv) = rest[5 * parts + 6 :]

    mem, gx, gy = lax.axis_index("mem"), lax.axis_index("gx"), lax.axis_index("gy")
    place, line = lax.rem(mem, inner), lax.div(mem, inner)
    near_x, near_y, diagonal = (mem, 1 - gx, gy), (mem, gx, 1 - gy), (mem, 1 - gx, 1 - gy)

    barrier = pltpu.get_barrier_semaphore()
    for peer in (near_x, near_y, diagonal):
        pl.semaphore_signal(barrier, inc=1, device_id=peer, device_id_type=MESH)
    for d in range(1, n):
        pl.semaphore_signal(
            barrier, inc=1, device_id=(lax.rem(mem + d, n), gx, gy), device_id_type=MESH
        )

    lane = lax.broadcasted_iota(jnp.int32, (1, count_y), 1)
    spot = lane & (STRIPE - 1)
    owner = lane >> 5
    group = spot >> 2
    packed_comp = jnp.where((group & 1) == 1, group >> 1, ((group >> 1) + 1) & 3)

    def seam_of(rows, size, comp):
        total = jnp.zeros((size, count_y), jnp.float32)
        for m in range(members):
            plane = force[m // 2, rows, :] if comp == 3 else old[m, comp, rows, :]
            low = roll_y(plane, 8 + STRIPE * m)
            high = roll_y(plane, 24 + STRIPE * m)
            total = jnp.where(owner == m, jnp.where(spot < 16, low, high), total)
        return total

    def load(i, carry):
        rows = pl.ds(pl.multiple_of(i * CHUNK, CHUNK), CHUNK)
        padded = pl.ds(pl.multiple_of(i * CHUNK + BASE, CHUNK), CHUNK)
        for m in range(members):
            for comp in range(3):
                old[m, comp, padded, :] = fields_ref[m, comp, rows, :]
        for p in range(pairs):
            force[p, padded, :] = noise_ref[p, rows, :]
        packed = jnp.zeros((CHUNK, count_y), jnp.float32)
        for comp in range(4):
            seam = seam_of(padded, CHUNK, comp)
            seam_own[comp, padded, :] = seam
            packed = jnp.where(packed_comp == comp, roll_y(seam, 8 * comp), packed)
        pack_out[rows, :] = packed
        return carry

    lax.fori_loop(0, count_x // CHUNK, load, 0)
    pl.semaphore_wait(barrier, n + 2)

    top = BASE + count_x
    first, last = pl.ds(0, EDGE), pl.ds(count_x - EDGE, EDGE)
    rim_low, rim_high = pl.ds(BASE - EDGE, EDGE), pl.ds(top, EDGE)
    moves = [
        (pack_out, pack_in.at[pl.ds(BASE, count_x), :], near_y),
        (fields_ref.at[:, :, last, :], old.at[:, :, rim_low, :], near_x),
        (fields_ref.at[:, :, first, :], old.at[:, :, rim_high, :], near_x),
        (noise_ref.at[:, last, :], force.at[:, rim_low, :], near_x),
        (noise_ref.at[:, first, :], force.at[:, rim_high, :], near_x),
        (pack_out.at[last, :], pack_in.at[rim_low, :], diagonal),
        (pack_out.at[first, :], pack_in.at[rim_high, :], diagonal),
    ]
    rims = []
    for k, (src, dst, peer) in enumerate(moves):
        rims.append(
            pltpu.make_async_remote_copy(
                src_ref=src,
                dst_ref=dst,
                send_sem=rim_send.at[k],
                recv_sem=rim_recv.at[k],
                device_id=peer,
                device_id_type=MESH,
            )
        )
    for copy in rims:
        copy.start()
    for copy in rims[1:5]:
        copy.wait_recv()

    total_y = 2 * count_y

    def turning(local):
        rows_y = lax.rem(gy * count_y + local + total_y, total_y)
        return 0.1 + 0.2 * ((rows_y.astype(jnp.float32) + 0.5) / total_y - 0.5)

    cor_tile = turning(lane)
    cor_seam = turning(jnp.where(spot < 16, spot - 8, spot - 24 + count_y))

    wide = (count_x + 2 * EDGE) // CHUNK

    def first_step(e):
        def body(i, carry):
            p, at = lax.div(i, wide), pl.multiple_of(lax.rem(i, wide) * CHUNK + EDGE, EDGE)
            m = 2 * p + e
            new = advance(
                lambda comp, d: old[m, comp, pl.ds(at + d, CHUNK), :],
                force[p, pl.ds(at, CHUNK), :],
                cor_tile,
            )
            for comp in range(3):
                mid[m, comp, pl.ds(at, CHUNK), :] = new[comp]
            return carry

        lax.fori_loop(0, pairs * wide, body, 0, unroll=3)

    first_step(0)

    for start in (BASE - EDGE, top):
        rows = pl.ds(start, EDGE)
        for comp in range(4):
            seam_own[comp, rows, :] = seam_of(rows, EDGE, comp)
    for copy in (rims[0], rims[5], rims[6]):
        copy.wait_recv()

    def seam_fill(i, carry):
        rows = pl.ds(pl.multiple_of(i * CHUNK + EDGE, EDGE), CHUNK)
        packed = pack_in[rows, :]
        for comp in range(4):
            seam_old[comp, rows, :] = jnp.where(
                (spot >= 8) & (spot < 24), seam_own[comp, rows, :], roll_y(packed, -8 * comp)
            )
        return carry

    lax.fori_loop(0, wide, seam_fill, 0)

    def seam_step(source, target):
        def body(i, carry):
            at = pl.multiple_of(i * CHUNK + EDGE, EDGE)
            new = advance(
                lambda comp, d: source[comp, pl.ds(at + d, CHUNK), :],
                seam_old[3, pl.ds(at, CHUNK), :],
                cor_seam,
            )
            for comp in range(3):
                target[comp, pl.ds(at, CHUNK), :] = new[comp]
            return carry

        lax.fori_loop(0, wide, body, 0, unroll=3)

    seam_step(seam_old, seam_mid)
    seam_step(seam_mid, seam_new)

    def z_copy(part, origin, right):
        way = 0 if right else 1
        peer = line + 1 if right else line - 1
        block = gathered[part].at[origin]
        return pltpu.make_async_remote_copy(
            src_ref=block,
            dst_ref=block,
            send_sem=z_send.at[way, part, origin],
            recv_sem=z_recv.at[way, part, origin],
            device_id=(peer * inner + place, gx, gy),
            device_id_type=MESH,
        )

    at_end = (line == 0) | (line == outer - 1)

    def start_own(part, when):
        go_right, go_left = line < outer - 2, line > 1
        if when is not None:
            go_right, go_left = go_right & when, go_left & when

        @pl.when(go_right)
        def _():
            z_copy(part, line, True).start()

        @pl.when(go_left)
        def _():
            z_copy(part, line, False).start()

    for e in range(2):
        if e == 1:
            first_step(1)
        for p in range(pairs):
            m = 2 * p + e

            def second_step(i, carry, m=m, p=p, e=e):
                row = pl.multiple_of(i * CHUNK, CHUNK)
                at = row + BASE
                new = advance(
                    lambda comp, d: mid[m, comp, pl.ds(at + d, CHUNK), :],
                    force[p, pl.ds(at, CHUNK), :],
                    cor_tile,
                )
                for comp in range(3):
                    seam = seam_new[comp, pl.ds(at, CHUNK), :]
                    low, high = roll_y(seam, -(STRIPE * m + 8)), roll_y(seam, -(STRIPE * m + 24))
                    whole = jnp.where(lane < 4, low, jnp.where(lane >= count_y - 4, high, new[comp]))
                    gathered[3 * e + comp][line, p, pl.ds(row, CHUNK), :] = whole
                return carry

            lax.fori_loop(0, count_x // CHUNK, second_step, 0, unroll=2)
        for comp in range(3):
            start_own(3 * e + comp, None if e == 0 else at_end)

    cells = cells_ref[...]
    hot_y = jnp.where(
        lax.broadcasted_iota(jnp.int32, (count_y, cells.shape[1]), 0) == lax.rem(cells, count_y),
        1.0,
        0.0,
    )
    hot_x = lax.broadcasted_iota(jnp.int32, (count_x, cells.shape[1]), 0) == lax.div(cells, count_y)
    tile_lane = lax.broadcasted_iota(jnp.int32, (8, 128), 1)
    own = jnp.zeros((8, 128), jnp.float32)
    for m in range(members):
        picked = jnp.dot(
            gathered[3 * (m % 2)][line, m // 2],
            hot_y,
            precision=lax.Precision.HIGHEST,
            preferred_element_type=jnp.float32,
        )
        seen = jnp.sum(jnp.where(hot_x, picked, 0.0), axis=0, keepdims=True)
        misfit = seen - values_ref[...]
        logw = -2.0 * jnp.sum(misfit * misfit, axis=1, keepdims=True)
        own = jnp.where(tile_lane == m, logw, own)
    logw_out[...] = own
    logw_all[mem] = own

    def w_copy(d):
        return pltpu.make_async_remote_copy(
            src_ref=logw_out,
            dst_ref=logw_all.at[mem],
            send_sem=w_send.at[d],
            recv_sem=w_recv.at[d],
            device_id=(lax.rem(mem + d, n), gx, gy),
            device_id_type=MESH,
        )

    for d in range(1, n):
        w_copy(d).start()

    def x_copy(part, d):
        return pltpu.make_async_remote_copy(
            src_ref=offered[part].at[d],
            dst_ref=taken[part].at[place],
            send_sem=x_send.at[part, d],
            recv_sem=x_recv.at[part, d],
            device_id=(line * inner + lax.rem(place + d, inner), gx, gy),
            device_id_type=MESH,
        )

    def finish(part):
        e, comp = part // 3, part % 3
        for d in range(1, inner):
            x_copy(part, d).wait_recv()
        for s in range(pairs):
            source = lax.rem(lax.div(anc_ref[0, mem * pairs + s], pairs), inner)
            out_ref[2 * s + e, comp] = taken[part][source, s]

    def end_copy(part):
        end = jnp.where(line == 1, 0, outer - 1)
        return pltpu.make_async_remote_copy(
            src_ref=end_out[part],
            dst_ref=end_in[part],
            send_sem=end_send.at[part],
            recv_sem=end_recv.at[part],
            device_id=(end * inner + place, gx, gy),
            device_id_type=MESH,
        )

    def pick(part, wanted):
        origin = lax.div(lax.div(wanted, pairs), inner)
        return gathered[part][origin, lax.rem(wanted, pairs)]

    def deliver(part):
        @pl.when((line == 1) | (line == outer - 2))
        def _():
            end = jnp.where(line == 1, 0, outer - 1)
            for k in range(inner * pairs):
                end_out[part][k] = pick(part, anc_ref[0, end * inner * pairs + k])
            end_copy(part).start()

        def place_block(d, s, block):
            if d == 0:
                taken[part][place, s] = block
            else:
                offered[part][d, s] = block

        @pl.when(jnp.logical_not(at_end))
        def _():
            for d in range(inner):
                goal = line * inner + lax.rem(place + d, inner)
                for s in range(pairs):
                    place_block(d, s, pick(part, anc_ref[0, goal * pairs + s]))

        @pl.when(at_end)
        def _():
            end_copy(part).wait_recv()
            for d in range(inner):
                spot_in = lax.rem(place + d, inner)
                for s in range(pairs):
                    wanted = anc_ref[0, (line * inner + spot_in) * pairs + s]
                    origin = lax.div(lax.div(wanted, pairs), inner)
                    here = gathered[part][line, 0]
                    for p in range(1, pairs):
                        here = jnp.where(lax.rem(wanted, pairs) == p, gathered[part][line, p], here)
                    sent = end_in[part][spot_in * pairs + s]
                    place_block(d, s, jnp.where(origin == line, here, sent))

        for d in range(1, inner):
            x_copy(part, d).start()

    middle = jnp.logical_not(at_end)
    for turn in range(parts + outer - 2):
        for t in range(1, outer):
            part = turn - (t - 1)
            if not 0 <= part < parts:
                continue

            @pl.when((line - t >= 0) & (line < outer - 1))
            def _(part=part, t=t):
                z_copy(part, line - t, True).wait_recv()

                @pl.when(line < outer - 2)
                def _():
                    z_copy(part, line - t, True).start()

            @pl.when((line + t < outer) & (line > 0))
            def _(part=part, t=t):
                z_copy(part, line + t, False).wait_recv()

                @pl.when(line > 1)
                def _():
                    z_copy(part, line + t, False).start()

            if t == 1 and part + 3 < parts:
                start_own(part + 3, middle)
        part = turn - (outer - 2)
        if part >= 0:
            deliver(part)
            if part > 0:
                finish(part - 1)
    finish(parts - 1)

    for d in range(1, n):
        w_copy(d).wait_recv()
    every = logw_all[...]
    real = lax.broadcasted_iota(jnp.int32, every.shape, 2) < members
    once = lax.broadcasted_iota(jnp.int32, every.shape, 1) == 0
    every_max = jnp.max(jnp.where(real, every, -jnp.inf), axis=0)
    peak = jnp.max(every_max, axis=1, keepdims=True)
    expo = jnp.where(real & once, jnp.exp(jnp.where(real, every - peak[None], 0.0)), 0.0)
    total = jnp.sum(jnp.sum(jnp.sum(expo, axis=0), axis=1, keepdims=True), axis=0, keepdims=True)
    normal = own - peak - jnp.log(total)
    weights_ref[...] = normal[0:1, 0:members]

    for copy in rims:
        copy.wait_send()
    for d in range(1, n):
        w_copy(d).wait_send()
    for part in range(parts):
        for d in range(1, inner):
            x_copy(part, d).wait_send()

        @pl.when((line == 1) | (line == outer - 2))
        def _(part=part):
            end_copy(part).wait_send()

        for t in range(outer):

            @pl.when((line - t >= 0) & (line < outer - 2))
            def _(part=part, t=t):
                z_copy(part, line - t, True).wait_send()

            @pl.when((line + t < outer) & (line > 1))
            def _(part=part, t=t):
                z_copy(part, line + t, False).wait_send()


def shards(n, fields, noise, ancestors, obs_cells, obs_values):
    members, comps, count_x, count_y = fields.shape
    inner = 1
    while inner * inner * 4 <= n:
        inner *= 2
    outer = n // inner
    pairs = members // 2
    rows = count_x + 2 * BASE
    f32 = jnp.float32
    vmem = pl.BlockSpec(memory_space=pltpu.VMEM)
    dma = pltpu.SemaphoreType.DMA
    parts = 2 * comps
    plane = (count_x, count_y)
    scratch = [
        pltpu.VMEM((members, 3, rows, count_y), f32),
        pltpu.VMEM((members, 3, rows, count_y), f32),
        pltpu.VMEM((pairs, rows, count_y), f32),
        pltpu.VMEM((4, rows, count_y), f32),
        pltpu.VMEM((4, rows, count_y), f32),
        pltpu.VMEM((3, rows, count_y), f32),
        pltpu.VMEM((3, rows, count_y), f32),
        pltpu.VMEM(plane, f32),
        pltpu.VMEM((rows, count_y), f32),
        pltpu.VMEM((8, 128), f32),
        pltpu.VMEM((n, 8, 128), f32),
    ]
    scratch += [pltpu.VMEM((outer, pairs) + plane, f32)] * parts
    scratch += [pltpu.VMEM((inner, pairs) + plane, f32)] * (2 * parts)
    scratch += [pltpu.VMEM((inner * pairs,) + plane, f32)] * (2 * parts)
    scratch += [
        dma((7,)),
        dma((7,)),
        dma((n,)),
        dma((n,)),
        dma((2, parts, outer)),
        dma((2, parts, outer)),
        dma((parts, inner)),
        dma((parts, inner)),
        dma((parts,)),
        dma((parts,)),
    ]
    resampled, weights = pl.pallas_call(
        functools.partial(kernel, (n, inner, outer, members, count_x, count_y)),
        out_shape=(
            jax.ShapeDtypeStruct(fields.shape, f32),
            jax.ShapeDtypeStruct((1, members), f32),
        ),
        in_specs=[vmem, vmem, pl.BlockSpec(memory_space=pltpu.SMEM), vmem, vmem],
        out_specs=(vmem, vmem),
        scratch_shapes=scratch,
        compiler_params=pltpu.CompilerParams(
            collective_id=0, has_side_effects=True, vmem_limit_bytes=48 * 1024 * 1024
        ),
    )(
        fields,
        noise,
        ancestors.reshape(1, -1),
        obs_cells.reshape(1, -1),
        obs_values.reshape(1, -1),
    )
    return resampled, weights.reshape(1, 1, members)


def solution(mesh):
    return jax.shard_map(
        functools.partial(shards, mesh.shape["mem"]),
        mesh=mesh,
        in_specs=(
            P("mem", None, "gx", "gy"),
            P("mem", "gx", "gy"),
            P("gx", "gy", None),
            P("gx", "gy", None),
            P("gx", "gy", None),
        ),
        out_specs=(P("mem", None, "gx", "gy"), P("gx", "gy", "mem")),
        check_vma=False,
    )
```

```python
import functools

import jax
import jax.numpy as jnp
from jax import lax
from jax.experimental import pallas as pl
from jax.experimental.pallas import tpu as pltpu
from jax.sharding import PartitionSpec as P

COURANT = 0.3
NOISE_AMP = 0.1
MESH = pl.DeviceIdType.MESH
BASE = 16
EDGE = 8
STRIPE = 32
CHUNK = 16
LEAD = 9


def roll_y(a, shift):
    return pltpu.roll(a, shift % a.shape[-1], 1)


def advance(get, force, coriolis):
    def parts(comp):
        mid, low, high = get(comp, 0), get(comp, -1), get(comp, 1)
        near = low + high
        far = get(comp, -2) + get(comp, 2)
        left, right = roll_y(mid, 1), roll_y(mid, -1)
        cross = 0.09 * mid - 0.01 * near
        smooth = (
            0.7 * mid
            + 0.09 * near
            - 0.005 * far
            + roll_y(cross - 0.005 * right, -1)
            + roll_y(cross - 0.005 * left, 1)
        )
        return mid, low, high, left, right, smooth

    _, eta_lo, eta_hi, eta_le, eta_ri, eta_s = parts(0)
    u, u_lo, u_hi, u_le, u_ri, u_s = parts(1)
    v, v_lo, v_hi, v_le, v_ri, v_s = parts(2)
    flux = (
        (1.0 + eta_hi) * u_hi
        - (1.0 + eta_lo) * u_lo
        + (1.0 + eta_ri) * v_ri
        - (1.0 + eta_le) * v_le
    )
    half = 0.5 * COURANT
    new_eta = eta_s - half * flux + NOISE_AMP * force
    turn = COURANT * coriolis
    new_u = u_s - half * (u * (u_hi - u_lo) + v * (u_ri - u_le) + (eta_hi - eta_lo)) + turn * v
    new_v = v_s - half * (u * (v_hi - v_lo) + v * (v_ri - v_le) + (eta_ri - eta_le)) - turn * u
    return new_eta, new_u, new_v


def kernel(
    cfg,
    fields_ref,
    noise_ref,
    anc_ref,
    cells_ref,
    values_ref,
    out_ref,
    weights_ref,
    old,
    mid,
    force,
    seam_own,
    seam_old,
    seam_mid,
    seam_new,
    pack_out,
    pack_in,
    logw_out,
    logw_all,
    *rest,
):
    n, inner, outer, members, count_x, count_y = cfg
    pairs = members // 2
    parts = 12
    strip = count_x // 2
    gathered = rest[0:parts]
    offered = rest[parts : 2 * parts]
    taken = rest[2 * parts : 3 * parts]
    end_out = rest[3 * parts : 4 * parts]
    end_in = rest[4 * parts : 5 * parts]
    (rim_send, rim_recv, w_send, w_recv, z_send, z_recv) = rest[5 * parts : 5 * parts + 6]
    (x_send, x_recv, end_send, end_recv) = rest[5 * parts + 6 :]

    mem, gx, gy = lax.axis_index("mem"), lax.axis_index("gx"), lax.axis_index("gy")
    place, line = lax.rem(mem, inner), lax.div(mem, inner)
    near_x, near_y, diagonal = (mem, 1 - gx, gy), (mem, gx, 1 - gy), (mem, 1 - gx, 1 - gy)

    barrier = pltpu.get_barrier_semaphore()
    for peer in (near_x, near_y, diagonal):
        pl.semaphore_signal(barrier, inc=1, device_id=peer, device_id_type=MESH)
    for d in range(1, n):
        pl.semaphore_signal(
            barrier, inc=1, device_id=(lax.rem(mem + d, n), gx, gy), device_id_type=MESH
        )

    lane = lax.broadcasted_iota(jnp.int32, (1, count_y), 1)
    spot = lane & (STRIPE - 1)
    owner = lane >> 5
    group = spot >> 2
    packed_comp = jnp.where((group & 1) == 1, group >> 1, ((group >> 1) + 1) & 3)

    def seam_of(rows, size, comp):
        total = jnp.zeros((size, count_y), jnp.float32)
        for m in range(members):
            plane = force[m // 2, rows, :] if comp == 3 else old[m, comp, rows, :]
            low = roll_y(plane, 8 + STRIPE * m)
            high = roll_y(plane, 24 + STRIPE * m)
            total = jnp.where(owner == m, jnp.where(spot < 16, low, high), total)
        return total

    def load(i, carry):
        rows = pl.ds(pl.multiple_of(i * CHUNK, CHUNK), CHUNK)
        padded = pl.ds(pl.multiple_of(i * CHUNK + BASE, CHUNK), CHUNK)
        for m in range(members):
            for comp in range(3):
                old[m, comp, padded, :] = fields_ref[m, comp, rows, :]
        for p in range(pairs):
            force[p, padded, :] = noise_ref[p, rows, :]
        packed = jnp.zeros((CHUNK, count_y), jnp.float32)
        for comp in range(4):
            seam = seam_of(padded, CHUNK, comp)
            seam_own[comp, padded, :] = seam
            packed = jnp.where(packed_comp == comp, roll_y(seam, 8 * comp), packed)
        pack_out[rows, :] = packed
        return carry

    lax.fori_loop(0, count_x // CHUNK, load, 0)
    pl.semaphore_wait(barrier, n + 2)

    top = BASE + count_x
    first, last = pl.ds(0, EDGE), pl.ds(count_x - EDGE, EDGE)
    rim_low, rim_high = pl.ds(BASE - EDGE, EDGE), pl.ds(top, EDGE)
    moves = [
        (pack_out, pack_in.at[pl.ds(BASE, count_x), :], near_y),
        (fields_ref.at[:, :, last, :], old.at[:, :, rim_low, :], near_x),
        (fields_ref.at[:, :, first, :], old.at[:, :, rim_high, :], near_x),
        (noise_ref.at[:, last, :], force.at[:, rim_low, :], near_x),
        (noise_ref.at[:, first, :], force.at[:, rim_high, :], near_x),
        (pack_out.at[last, :], pack_in.at[rim_low, :], diagonal),
        (pack_out.at[first, :], pack_in.at[rim_high, :], diagonal),
    ]
    rims = []
    for k, (src, dst, peer) in enumerate(moves):
        rims.append(
            pltpu.make_async_remote_copy(
                src_ref=src,
                dst_ref=dst,
                send_sem=rim_send.at[k],
                recv_sem=rim_recv.at[k],
                device_id=peer,
                device_id_type=MESH,
            )
        )
    for copy in rims:
        copy.start()
    total_y = 2 * count_y

    def turning(local):
        rows_y = lax.rem(gy * count_y + local + total_y, total_y)
        return 0.1 + 0.2 * ((rows_y.astype(jnp.float32) + 0.5) / total_y - 0.5)

    cor_tile = turning(lane)
    cor_seam = turning(jnp.where(spot < 16, spot - 8, spot - 24 + count_y))

    wide = (count_x + 2 * EDGE) // CHUNK

    def first_step(e, low, stride, count):
        def body(i, carry):
            p, k = lax.div(i, count), lax.rem(i, count) * stride + low
            at = pl.multiple_of(k * CHUNK + EDGE, EDGE)
            m = 2 * p + e
            new = advance(
                lambda comp, d: old[m, comp, pl.ds(at + d, CHUNK), :],
                force[p, pl.ds(at, CHUNK), :],
                cor_tile,
            )
            for comp in range(3):
                mid[m, comp, pl.ds(at, CHUNK), :] = new[comp]
            return carry

        lax.fori_loop(0, pairs * count, body, 0, unroll=2)

    first_step(0, 1, 1, wide - 2)
    for copy in rims[1:5]:
        copy.wait_recv()
    first_step(0, 0, wide - 1, 2)

    for start in (BASE - EDGE, top):
        rows = pl.ds(start, EDGE)
        for comp in range(4):
            seam_own[comp, rows, :] = seam_of(rows, EDGE, comp)
    for copy in (rims[0], rims[5], rims[6]):
        copy.wait_recv()

    def seam_fill(i, carry):
        rows = pl.ds(pl.multiple_of(i * CHUNK + EDGE, EDGE), CHUNK)
        packed = pack_in[rows, :]
        for comp in range(4):
            seam_old[comp, rows, :] = jnp.where(
                (spot >= 8) & (spot < 24), seam_own[comp, rows, :], roll_y(packed, -8 * comp)
            )
        return carry

    lax.fori_loop(0, wide, seam_fill, 0)

    def seam_step(source, target):
        def body(i, carry):
            at = pl.multiple_of(i * CHUNK + EDGE, EDGE)
            new = advance(
                lambda comp, d: source[comp, pl.ds(at + d, CHUNK), :],
                seam_old[3, pl.ds(at, CHUNK), :],
                cor_seam,
            )
            for comp in range(3):
                target[comp, pl.ds(at, CHUNK), :] = new[comp]
            return carry

        lax.fori_loop(0, wide, body, 0, unroll=3)

    seam_step(seam_old, seam_mid)
    seam_step(seam_mid, seam_new)

    def z_copy(part, origin, right):
        way = 0 if right else 1
        peer = line + 1 if right else line - 1
        block = gathered[part].at[origin]
        return pltpu.make_async_remote_copy(
            src_ref=block,
            dst_ref=block,
            send_sem=z_send.at[way, part, origin],
            recv_sem=z_recv.at[way, part, origin],
            device_id=(peer * inner + place, gx, gy),
            device_id_type=MESH,
        )

    at_end = (line == 0) | (line == outer - 1)

    def start_own(part, when):
        go_right, go_left = line < outer - 2, line > 1
        if when is not None:
            go_right, go_left = go_right & when, go_left & when

        @pl.when(go_right)
        def _():
            z_copy(part, line, True).start()

        @pl.when(go_left)
        def _():
            z_copy(part, line, False).start()

    for e in range(2):
        if e == 1:
            first_step(1, 0, 1, wide)
        for half in range(2):

            def second_step(i, carry, e=e, half=half):
                p = lax.div(i, strip // CHUNK)
                m = 2 * p + e
                row = pl.multiple_of(lax.rem(i, strip // CHUNK) * CHUNK, CHUNK)
                at = row + (BASE + half * strip)
                new = advance(
                    lambda comp, d: mid[m, comp, pl.ds(at + d, CHUNK), :],
                    force[p, pl.ds(at, CHUNK), :],
                    cor_tile,
                )
                for comp in range(3):
                    seam = seam_new[comp, pl.ds(at, CHUNK), :]
                    low, high = jnp.zeros_like(seam), jnp.zeros_like(seam)
                    for q in range(pairs):
                        base = STRIPE * (2 * q + e)
                        low = jnp.where(p == q, roll_y(seam, -(base + 8)), low)
                        high = jnp.where(p == q, roll_y(seam, -(base + 24)), high)
                    whole = jnp.where(lane < 4, low, jnp.where(lane >= count_y - 4, high, new[comp]))
                    gathered[6 * e + 3 * half + comp][line, p, pl.ds(row, CHUNK), :] = whole
                return carry

            lax.fori_loop(0, pairs * (strip // CHUNK), second_step, 0, unroll=2)
            for comp in range(3):
                part = 6 * e + 3 * half + comp
                start_own(part, None if part < LEAD else at_end)

    def x_copy(part, d):
        return pltpu.make_async_remote_copy(
            src_ref=offered[part].at[d],
            dst_ref=taken[part].at[place],
            send_sem=x_send.at[part, d],
            recv_sem=x_recv.at[part, d],
            device_id=(line * inner + lax.rem(place + d, inner), gx, gy),
            device_id_type=MESH,
        )

    def finish(part):
        e, rows, comp = part // 6, pl.ds(part // 3 % 2 * strip, strip), part % 3
        for d in range(1, inner):
            x_copy(part, d).wait_recv()
        for s in range(pairs):
            source = lax.rem(lax.div(anc_ref[0, mem * pairs + s], pairs), inner)
            out_ref[2 * s + e, comp, rows, :] = taken[part][source, s]

    def end_copy(part):
        end = jnp.where(line == 1, 0, outer - 1)
        return pltpu.make_async_remote_copy(
            src_ref=end_out[part],
            dst_ref=end_in[part],
            send_sem=end_send.at[part],
            recv_sem=end_recv.at[part],
            device_id=(end * inner + place, gx, gy),
            device_id_type=MESH,
        )

    def pick(part, wanted):
        origin = lax.div(lax.div(wanted, pairs), inner)
        return gathered[part][origin, lax.rem(wanted, pairs)]

    def deliver(part):
        @pl.when((line == 1) | (line == outer - 2))
        def _():
            end = jnp.where(line == 1, 0, outer - 1)
            for k in range(inner * pairs):
                end_out[part][k] = pick(part, anc_ref[0, end * inner * pairs + k])
            end_copy(part).start()

        def place_block(d, s, block):
            if d == 0:
                taken[part][place, s] = block
            else:
                offered[part][d, s] = block

        @pl.when(jnp.logical_not(at_end))
        def _():
            for d in range(inner):
                goal = line * inner + lax.rem(place + d, inner)
                for s in range(pairs):
                    place_block(d, s, pick(part, anc_ref[0, goal * pairs + s]))

        @pl.when(at_end)
        def _():
            end_copy(part).wait_recv()
            for d in range(inner):
                spot_in = lax.rem(place + d, inner)
                for s in range(pairs):
                    wanted = anc_ref[0, (line * inner + spot_in) * pairs + s]
                    origin = lax.div(lax.div(wanted, pairs), inner)
                    here = gathered[part][line, 0]
                    for p in range(1, pairs):
                        here = jnp.where(lax.rem(wanted, pairs) == p, gathered[part][line, p], here)
                    sent = end_in[part][spot_in * pairs + s]
                    place_block(d, s, jnp.where(origin == line, here, sent))

        for d in range(1, inner):
            x_copy(part, d).start()

    def w_copy(d):
        return pltpu.make_async_remote_copy(
            src_ref=logw_out,
            dst_ref=logw_all.at[mem],
            send_sem=w_send.at[d],
            recv_sem=w_recv.at[d],
            device_id=(lax.rem(mem + d, n), gx, gy),
            device_id_type=MESH,
        )

    def weigh():
        cells = cells_ref[...]
        hot_y = jnp.where(
            lax.broadcasted_iota(jnp.int32, (count_y, cells.shape[1]), 0) == lax.rem(cells, count_y),
            1.0,
            0.0,
        )
        hot_x = lax.broadcasted_iota(jnp.int32, (count_x, cells.shape[1]), 0) == lax.div(cells, count_y)
        tile_lane = lax.broadcasted_iota(jnp.int32, (8, 128), 1)
        own = jnp.zeros((8, 128), jnp.float32)
        for m in range(members):
            seen = jnp.zeros(cells.shape, jnp.float32)
            for half in range(2):
                picked = jnp.dot(
                    gathered[6 * (m % 2) + 3 * half][line, m // 2],
                    hot_y,
                    precision=lax.Precision.HIGHEST,
                    preferred_element_type=jnp.float32,
                )
                here = hot_x[half * strip : (half + 1) * strip]
                seen += jnp.sum(jnp.where(here, picked, 0.0), axis=0, keepdims=True)
            misfit = seen - values_ref[...]
            logw = -2.0 * jnp.sum(misfit * misfit, axis=1, keepdims=True)
            own = jnp.where(tile_lane == m, logw, own)
        logw_out[...] = own
        logw_all[mem] = own
        for d in range(1, n):
            w_copy(d).start()

    middle = jnp.logical_not(at_end)
    for turn in range(parts + outer - 2):
        for t in range(1, outer):
            part = turn - (t - 1)
            if not 0 <= part < parts:
                continue

            @pl.when((line - t >= 0) & (line < outer - 1))
            def _(part=part, t=t):
                z_copy(part, line - t, True).wait_recv()

                @pl.when(line < outer - 2)
                def _():
                    z_copy(part, line - t, True).start()

            @pl.when((line + t < outer) & (line > 0))
            def _(part=part, t=t):
                z_copy(part, line + t, False).wait_recv()

                @pl.when(line > 1)
                def _():
                    z_copy(part, line + t, False).start()

            if t == 1 and part + LEAD < parts:
                start_own(part + LEAD, middle)
        if turn == 2:
            weigh()
        part = turn - (outer - 2)
        if part >= 0:
            deliver(part)
            if part > 0:
                finish(part - 1)
    finish(parts - 1)

    for d in range(1, n):
        w_copy(d).wait_recv()
    every = logw_all[...]
    real = lax.broadcasted_iota(jnp.int32, every.shape, 2) < members
    once = lax.broadcasted_iota(jnp.int32, every.shape, 1) == 0
    every_max = jnp.max(jnp.where(real, every, -jnp.inf), axis=0)
    peak = jnp.max(every_max, axis=1, keepdims=True)
    expo = jnp.where(real & once, jnp.exp(jnp.where(real, every - peak[None], 0.0)), 0.0)
    total = jnp.sum(jnp.sum(jnp.sum(expo, axis=0), axis=1, keepdims=True), axis=0, keepdims=True)
    normal = logw_out[...] - peak - jnp.log(total)
    weights_ref[...] = normal[0:1, 0:members]

    for copy in rims:
        copy.wait_send()
    for d in range(1, n):
        w_copy(d).wait_send()
    for part in range(parts):
        for d in range(1, inner):
            x_copy(part, d).wait_send()

        @pl.when((line == 1) | (line == outer - 2))
        def _(part=part):
            end_copy(part).wait_send()

        for t in range(outer):

            @pl.when((line - t >= 0) & (line < outer - 2))
            def _(part=part, t=t):
                z_copy(part, line - t, True).wait_send()

            @pl.when((line + t < outer) & (line > 1))
            def _(part=part, t=t):
                z_copy(part, line + t, False).wait_send()


def shards(n, fields, noise, ancestors, obs_cells, obs_values):
    members, comps, count_x, count_y = fields.shape
    inner = 1
    while inner * inner * 4 <= n:
        inner *= 2
    outer = n // inner
    pairs = members // 2
    rows = count_x + 2 * BASE
    f32 = jnp.float32
    vmem = pl.BlockSpec(memory_space=pltpu.VMEM)
    dma = pltpu.SemaphoreType.DMA
    parts = 4 * comps
    plane = (count_x // 2, count_y)
    scratch = [
        pltpu.VMEM((members, 3, rows, count_y), f32),
        pltpu.VMEM((members, 3, rows, count_y), f32),
        pltpu.VMEM((pairs, rows, count_y), f32),
        pltpu.VMEM((4, rows, count_y), f32),
        pltpu.VMEM((4, rows, count_y), f32),
        pltpu.VMEM((3, rows, count_y), f32),
        pltpu.VMEM((3, rows, count_y), f32),
        pltpu.VMEM((count_x, count_y), f32),
        pltpu.VMEM((rows, count_y), f32),
        pltpu.VMEM((8, 128), f32),
        pltpu.VMEM((n, 8, 128), f32),
    ]
    scratch += [pltpu.VMEM((outer, pairs) + plane, f32)] * parts
    scratch += [pltpu.VMEM((inner, pairs) + plane, f32)] * (2 * parts)
    scratch += [pltpu.VMEM((inner * pairs,) + plane, f32)] * (2 * parts)
    scratch += [
        dma((7,)),
        dma((7,)),
        dma((n,)),
        dma((n,)),
        dma((2, parts, outer)),
        dma((2, parts, outer)),
        dma((parts, inner)),
        dma((parts, inner)),
        dma((parts,)),
        dma((parts,)),
    ]
    resampled, weights = pl.pallas_call(
        functools.partial(kernel, (n, inner, outer, members, count_x, count_y)),
        out_shape=(
            jax.ShapeDtypeStruct(fields.shape, f32),
            jax.ShapeDtypeStruct((1, members), f32),
        ),
        in_specs=[vmem, vmem, pl.BlockSpec(memory_space=pltpu.SMEM), vmem, vmem],
        out_specs=(vmem, vmem),
        scratch_shapes=scratch,
        compiler_params=pltpu.CompilerParams(
            collective_id=0, has_side_effects=True, vmem_limit_bytes=48 * 1024 * 1024
        ),
    )(
        fields,
        noise,
        ancestors.reshape(1, -1),
        obs_cells.reshape(1, -1),
        obs_values.reshape(1, -1),
    )
    return resampled, weights.reshape(1, 1, members)


def solution(mesh):
    return jax.shard_map(
        functools.partial(shards, mesh.shape["mem"]),
        mesh=mesh,
        in_specs=(
            P("mem", None, "gx", "gy"),
            P("mem", "gx", "gy"),
            P("gx", "gy", None),
            P("gx", "gy", None),
            P("gx", "gy", None),
        ),
        out_specs=(P("mem", None, "gx", "gy"), P("gx", "gy", "mem")),
        check_vma=False,
    )
```

```python
import functools

import jax
import jax.numpy as jnp
from jax import lax
from jax.experimental import pallas as pl
from jax.experimental.pallas import tpu as pltpu
from jax.sharding import PartitionSpec as P

COURANT = 0.3
NOISE_AMP = 0.1
MESH = pl.DeviceIdType.MESH
BASE = 16
EDGE = 8
STRIPE = 32
CHUNK = 16
LEAD = 5


def roll_y(a, shift):
    return pltpu.roll(a, shift % a.shape[-1], 1)


def advance(get, force, coriolis):
    def parts(comp):
        mid, low, high = get(comp, 0), get(comp, -1), get(comp, 1)
        near = low + high
        far = get(comp, -2) + get(comp, 2)
        left, right = roll_y(mid, 1), roll_y(mid, -1)
        cross = 0.09 * mid - 0.01 * near
        smooth = (
            0.7 * mid
            + 0.09 * near
            - 0.005 * far
            + roll_y(cross - 0.005 * right, -1)
            + roll_y(cross - 0.005 * left, 1)
        )
        return mid, low, high, left, right, smooth

    _, eta_lo, eta_hi, eta_le, eta_ri, eta_s = parts(0)
    u, u_lo, u_hi, u_le, u_ri, u_s = parts(1)
    v, v_lo, v_hi, v_le, v_ri, v_s = parts(2)
    flux = (
        (1.0 + eta_hi) * u_hi
        - (1.0 + eta_lo) * u_lo
        + (1.0 + eta_ri) * v_ri
        - (1.0 + eta_le) * v_le
    )
    half = 0.5 * COURANT
    new_eta = eta_s - half * flux + NOISE_AMP * force
    turn = COURANT * coriolis
    new_u = u_s - half * (u * (u_hi - u_lo) + v * (u_ri - u_le) + (eta_hi - eta_lo)) + turn * v
    new_v = v_s - half * (u * (v_hi - v_lo) + v * (v_ri - v_le) + (eta_ri - eta_le)) - turn * u
    return new_eta, new_u, new_v


def kernel(
    cfg,
    fields_ref,
    noise_ref,
    anc_ref,
    cells_ref,
    values_ref,
    out_ref,
    weights_ref,
    old,
    mid,
    force,
    seam_own,
    seam_old,
    seam_mid,
    seam_new,
    pack_out,
    pack_in,
    logw_out,
    logw_all,
    *rest,
):
    n, inner, outer, members, count_x, count_y = cfg
    pairs = members // 2
    parts = 6
    gathered = rest[0:parts]
    offered = rest[parts : 2 * parts]
    taken = rest[2 * parts : 3 * parts]
    end_out = rest[3 * parts : 4 * parts]
    end_in = rest[4 * parts : 5 * parts]
    (rim_send, rim_recv, w_send, w_recv, z_send, z_recv) = rest[5 * parts : 5 * parts + 6]
    (x_send, x_recv, end_send, end_recv) = rest[5 * parts + 6 :]

    mem, gx, gy = lax.axis_index("mem"), lax.axis_index("gx"), lax.axis_index("gy")
    place, line = lax.rem(mem, inner), lax.div(mem, inner)
    near_x, near_y, diagonal = (mem, 1 - gx, gy), (mem, gx, 1 - gy), (mem, 1 - gx, 1 - gy)

    barrier = pltpu.get_barrier_semaphore()
    for peer in (near_x, near_y, diagonal):
        pl.semaphore_signal(barrier, inc=1, device_id=peer, device_id_type=MESH)
    for d in range(1, n):
        pl.semaphore_signal(
            barrier, inc=1, device_id=(lax.rem(mem + d, n), gx, gy), device_id_type=MESH
        )

    lane = lax.broadcasted_iota(jnp.int32, (1, count_y), 1)
    spot = lane & (STRIPE - 1)
    owner = lane >> 5
    group = spot >> 2
    packed_comp = jnp.where((group & 1) == 1, group >> 1, ((group >> 1) + 1) & 3)

    def seam_of(rows, size, comp):
        total = jnp.zeros((size, count_y), jnp.float32)
        for m in range(members):
            plane = force[m // 2, rows, :] if comp == 3 else old[m, comp, rows, :]
            low = roll_y(plane, 8 + STRIPE * m)
            high = roll_y(plane, 24 + STRIPE * m)
            total = jnp.where(owner == m, jnp.where(spot < 16, low, high), total)
        return total

    def load(i, carry):
        rows = pl.ds(pl.multiple_of(i * CHUNK, CHUNK), CHUNK)
        padded = pl.ds(pl.multiple_of(i * CHUNK + BASE, CHUNK), CHUNK)
        for m in range(members):
            for comp in range(3):
                old[m, comp, padded, :] = fields_ref[m, comp, rows, :]
        for p in range(pairs):
            force[p, padded, :] = noise_ref[p, rows, :]
        packed = jnp.zeros((CHUNK, count_y), jnp.float32)
        for comp in range(4):
            seam = seam_of(padded, CHUNK, comp)
            seam_own[comp, padded, :] = seam
            packed = jnp.where(packed_comp == comp, roll_y(seam, 8 * comp), packed)
        pack_out[rows, :] = packed
        return carry

    lax.fori_loop(0, count_x // CHUNK, load, 0)
    pl.semaphore_wait(barrier, n + 2)

    top = BASE + count_x
    first, last = pl.ds(0, EDGE), pl.ds(count_x - EDGE, EDGE)
    rim_low, rim_high = pl.ds(BASE - EDGE, EDGE), pl.ds(top, EDGE)
    moves = [
        (pack_out, pack_in.at[pl.ds(BASE, count_x), :], near_y),
        (fields_ref.at[:, :, last, :], old.at[:, :, rim_low, :], near_x),
        (fields_ref.at[:, :, first, :], old.at[:, :, rim_high, :], near_x),
        (noise_ref.at[:, last, :], force.at[:, rim_low, :], near_x),
        (noise_ref.at[:, first, :], force.at[:, rim_high, :], near_x),
        (pack_out.at[last, :], pack_in.at[rim_low, :], diagonal),
        (pack_out.at[first, :], pack_in.at[rim_high, :], diagonal),
    ]
    rims = []
    for k, (src, dst, peer) in enumerate(moves):
        rims.append(
            pltpu.make_async_remote_copy(
                src_ref=src,
                dst_ref=dst,
                send_sem=rim_send.at[k],
                recv_sem=rim_recv.at[k],
                device_id=peer,
                device_id_type=MESH,
            )
        )
    for copy in rims:
        copy.start()
    for copy in rims[1:5]:
        copy.wait_recv()

    total_y = 2 * count_y

    def turning(local):
        rows_y = lax.rem(gy * count_y + local + total_y, total_y)
        return 0.1 + 0.2 * ((rows_y.astype(jnp.float32) + 0.5) / total_y - 0.5)

    cor_tile = turning(lane)
    cor_seam = turning(jnp.where(spot < 16, spot - 8, spot - 24 + count_y))

    wide = (count_x + 2 * EDGE) // CHUNK

    def first_step(e):
        def body(i, carry):
            p, at = lax.div(i, wide), pl.multiple_of(lax.rem(i, wide) * CHUNK + EDGE, EDGE)
            m = 2 * p + e
            new = advance(
                lambda comp, d: old[m, comp, pl.ds(at + d, CHUNK), :],
                force[p, pl.ds(at, CHUNK), :],
                cor_tile,
            )
            for comp in range(3):
                mid[m, comp, pl.ds(at, CHUNK), :] = new[comp]
            return carry

        lax.fori_loop(0, pairs * wide, body, 0, unroll=3)

    first_step(0)

    for start in (BASE - EDGE, top):
        rows = pl.ds(start, EDGE)
        for comp in range(4):
            seam_own[comp, rows, :] = seam_of(rows, EDGE, comp)
    for copy in (rims[0], rims[5], rims[6]):
        copy.wait_recv()

    def seam_fill(i, carry):
        rows = pl.ds(pl.multiple_of(i * CHUNK + EDGE, EDGE), CHUNK)
        packed = pack_in[rows, :]
        for comp in range(4):
            seam_old[comp, rows, :] = jnp.where(
                (spot >= 8) & (spot < 24), seam_own[comp, rows, :], roll_y(packed, -8 * comp)
            )
        return carry

    lax.fori_loop(0, wide, seam_fill, 0)

    def seam_step(source, target):
        def body(i, carry):
            at = pl.multiple_of(i * CHUNK + EDGE, EDGE)
            new = advance(
                lambda comp, d: source[comp, pl.ds(at + d, CHUNK), :],
                seam_old[3, pl.ds(at, CHUNK), :],
                cor_seam,
            )
            for comp in range(3):
                target[comp, pl.ds(at, CHUNK), :] = new[comp]
            return carry

        lax.fori_loop(0, wide, body, 0, unroll=3)

    seam_step(seam_old, seam_mid)
    seam_step(seam_mid, seam_new)

    def z_copy(part, origin, right):
        way = 0 if right else 1
        peer = line + 1 if right else line - 1
        block = gathered[part].at[origin]
        return pltpu.make_async_remote_copy(
            src_ref=block,
            dst_ref=block,
            send_sem=z_send.at[way, part, origin],
            recv_sem=z_recv.at[way, part, origin],
            device_id=(peer * inner + place, gx, gy),
            device_id_type=MESH,
        )

    at_end = (line == 0) | (line == outer - 1)

    def start_own(part, when):
        go_right, go_left = line < outer - 2, line > 1
        if when is not None:
            go_right, go_left = go_right & when, go_left & when

        @pl.when(go_right)
        def _():
            z_copy(part, line, True).start()

        @pl.when(go_left)
        def _():
            z_copy(part, line, False).start()

    for e in range(2):
        if e == 1:
            first_step(1)
        for p in range(pairs):
            m = 2 * p + e

            def second_step(i, carry, m=m, p=p, e=e):
                row = pl.multiple_of(i * CHUNK, CHUNK)
                at = row + BASE
                new = advance(
                    lambda comp, d: mid[m, comp, pl.ds(at + d, CHUNK), :],
                    force[p, pl.ds(at, CHUNK), :],
                    cor_tile,
                )
                for comp in range(3):
                    seam = seam_new[comp, pl.ds(at, CHUNK), :]
                    low, high = roll_y(seam, -(STRIPE * m + 8)), roll_y(seam, -(STRIPE * m + 24))
                    whole = jnp.where(lane < 4, low, jnp.where(lane >= count_y - 4, high, new[comp]))
                    gathered[3 * e + comp][line, p, pl.ds(row, CHUNK), :] = whole
                return carry

            lax.fori_loop(0, count_x // CHUNK, second_step, 0, unroll=2)
        for comp in range(3):
            start_own(3 * e + comp, None if 3 * e + comp < LEAD else at_end)

    cells = cells_ref[...]
    hot_y = jnp.where(
        lax.broadcasted_iota(jnp.int32, (count_y, cells.shape[1]), 0) == lax.rem(cells, count_y),
        1.0,
        0.0,
    )
    hot_x = lax.broadcasted_iota(jnp.int32, (count_x, cells.shape[1]), 0) == lax.div(cells, count_y)
    tile_lane = lax.broadcasted_iota(jnp.int32, (8, 128), 1)
    own = jnp.zeros((8, 128), jnp.float32)
    for m in range(members):
        picked = jnp.dot(
            gathered[3 * (m % 2)][line, m // 2],
            hot_y,
            precision=lax.Precision.HIGHEST,
            preferred_element_type=jnp.float32,
        )
        seen = jnp.sum(jnp.where(hot_x, picked, 0.0), axis=0, keepdims=True)
        misfit = seen - values_ref[...]
        logw = -2.0 * jnp.sum(misfit * misfit, axis=1, keepdims=True)
        own = jnp.where(tile_lane == m, logw, own)
    logw_out[...] = own
    logw_all[mem] = own

    def w_copy(d):
        return pltpu.make_async_remote_copy(
            src_ref=logw_out,
            dst_ref=logw_all.at[mem],
            send_sem=w_send.at[d],
            recv_sem=w_recv.at[d],
            device_id=(lax.rem(mem + d, n), gx, gy),
            device_id_type=MESH,
        )

    for d in range(1, n):
        w_copy(d).start()

    def x_copy(part, d):
        return pltpu.make_async_remote_copy(
            src_ref=offered[part].at[d],
            dst_ref=taken[part].at[place],
            send_sem=x_send.at[part, d],
            recv_sem=x_recv.at[part, d],
            device_id=(line * inner + lax.rem(place + d, inner), gx, gy),
            device_id_type=MESH,
        )

    def finish(part):
        e, comp = part // 3, part % 3
        for d in range(1, inner):
            x_copy(part, d).wait_recv()
        for s in range(pairs):
            source = lax.rem(lax.div(anc_ref[0, mem * pairs + s], pairs), inner)
            out_ref[2 * s + e, comp] = taken[part][source, s]

    def end_copy(part):
        end = jnp.where(line == 1, 0, outer - 1)
        return pltpu.make_async_remote_copy(
            src_ref=end_out[part],
            dst_ref=end_in[part],
            send_sem=end_send.at[part],
            recv_sem=end_recv.at[part],
            device_id=(end * inner + place, gx, gy),
            device_id_type=MESH,
        )

    def pick(part, wanted):
        origin = lax.div(lax.div(wanted, pairs), inner)
        return gathered[part][origin, lax.rem(wanted, pairs)]

    def deliver(part):
        @pl.when((line == 1) | (line == outer - 2))
        def _():
            end = jnp.where(line == 1, 0, outer - 1)
            for k in range(inner * pairs):
                end_out[part][k] = pick(part, anc_ref[0, end * inner * pairs + k])
            end_copy(part).start()

        def place_block(d, s, block):
            if d == 0:
                taken[part][place, s] = block
            else:
                offered[part][d, s] = block

        @pl.when(jnp.logical_not(at_end))
        def _():
            for d in range(inner):
                goal = line * inner + lax.rem(place + d, inner)
                for s in range(pairs):
                    place_block(d, s, pick(part, anc_ref[0, goal * pairs + s]))

        @pl.when(at_end)
        def _():
            end_copy(part).wait_recv()
            for d in range(inner):
                spot_in = lax.rem(place + d, inner)
                for s in range(pairs):
                    wanted = anc_ref[0, (line * inner + spot_in) * pairs + s]
                    origin = lax.div(lax.div(wanted, pairs), inner)
                    here = gathered[part][line, 0]
                    for p in range(1, pairs):
                        here = jnp.where(lax.rem(wanted, pairs) == p, gathered[part][line, p], here)
                    sent = end_in[part][spot_in * pairs + s]
                    place_block(d, s, jnp.where(origin == line, here, sent))

        for d in range(1, inner):
            x_copy(part, d).start()

    middle = jnp.logical_not(at_end)
    for turn in range(parts + outer - 2):
        for t in range(1, outer):
            part = turn - (t - 1)
            if not 0 <= part < parts:
                continue

            @pl.when((line - t >= 0) & (line < outer - 1))
            def _(part=part, t=t):
                z_copy(part, line - t, True).wait_recv()

                @pl.when(line < outer - 2)
                def _():
                    z_copy(part, line - t, True).start()

            @pl.when((line + t < outer) & (line > 0))
            def _(part=part, t=t):
                z_copy(part, line + t, False).wait_recv()

                @pl.when(line > 1)
                def _():
                    z_copy(part, line + t, False).start()

            if t == 1 and LEAD <= part + 3 < parts:
                start_own(part + 3, middle)
        part = turn - (outer - 2)
        if part >= 0:
            deliver(part)
            if part > 0:
                finish(part - 1)
    finish(parts - 1)

    for d in range(1, n):
        w_copy(d).wait_recv()
    every = logw_all[...]
    real = lax.broadcasted_iota(jnp.int32, every.shape, 2) < members
    once = lax.broadcasted_iota(jnp.int32, every.shape, 1) == 0
    every_max = jnp.max(jnp.where(real, every, -jnp.inf), axis=0)
    peak = jnp.max(every_max, axis=1, keepdims=True)
    expo = jnp.where(real & once, jnp.exp(jnp.where(real, every - peak[None], 0.0)), 0.0)
    total = jnp.sum(jnp.sum(jnp.sum(expo, axis=0), axis=1, keepdims=True), axis=0, keepdims=True)
    normal = own - peak - jnp.log(total)
    weights_ref[...] = normal[0:1, 0:members]

    for copy in rims:
        copy.wait_send()
    for d in range(1, n):
        w_copy(d).wait_send()
    for part in range(parts):
        for d in range(1, inner):
            x_copy(part, d).wait_send()

        @pl.when((line == 1) | (line == outer - 2))
        def _(part=part):
            end_copy(part).wait_send()

        for t in range(outer):

            @pl.when((line - t >= 0) & (line < outer - 2))
            def _(part=part, t=t):
                z_copy(part, line - t, True).wait_send()

            @pl.when((line + t < outer) & (line > 1))
            def _(part=part, t=t):
                z_copy(part, line + t, False).wait_send()


def shards(n, fields, noise, ancestors, obs_cells, obs_values):
    members, comps, count_x, count_y = fields.shape
    inner = 1
    while inner * inner * 4 <= n:
        inner *= 2
    outer = n // inner
    pairs = members // 2
    rows = count_x + 2 * BASE
    f32 = jnp.float32
    vmem = pl.BlockSpec(memory_space=pltpu.VMEM)
    dma = pltpu.SemaphoreType.DMA
    parts = 2 * comps
    plane = (count_x, count_y)
    scratch = [
        pltpu.VMEM((members, 3, rows, count_y), f32),
        pltpu.VMEM((members, 3, rows, count_y), f32),
        pltpu.VMEM((pairs, rows, count_y), f32),
        pltpu.VMEM((4, rows, count_y), f32),
        pltpu.VMEM((4, rows, count_y), f32),
        pltpu.VMEM((3, rows, count_y), f32),
        pltpu.VMEM((3, rows, count_y), f32),
        pltpu.VMEM(plane, f32),
        pltpu.VMEM((rows, count_y), f32),
        pltpu.VMEM((8, 128), f32),
        pltpu.VMEM((n, 8, 128), f32),
    ]
    scratch += [pltpu.VMEM((outer, pairs) + plane, f32)] * parts
    scratch += [pltpu.VMEM((inner, pairs) + plane, f32)] * (2 * parts)
    scratch += [pltpu.VMEM((inner * pairs,) + plane, f32)] * (2 * parts)
    scratch += [
        dma((7,)),
        dma((7,)),
        dma((n,)),
        dma((n,)),
        dma((2, parts, outer)),
        dma((2, parts, outer)),
        dma((parts, inner)),
        dma((parts, inner)),
        dma((parts,)),
        dma((parts,)),
    ]
    resampled, weights = pl.pallas_call(
        functools.partial(kernel, (n, inner, outer, members, count_x, count_y)),
        out_shape=(
            jax.ShapeDtypeStruct(fields.shape, f32),
            jax.ShapeDtypeStruct((1, members), f32),
        ),
        in_specs=[vmem, vmem, pl.BlockSpec(memory_space=pltpu.SMEM), vmem, vmem],
        out_specs=(vmem, vmem),
        scratch_shapes=scratch,
        compiler_params=pltpu.CompilerParams(
            collective_id=0, has_side_effects=True, vmem_limit_bytes=48 * 1024 * 1024
        ),
    )(
        fields,
        noise,
        ancestors.reshape(1, -1),
        obs_cells.reshape(1, -1),
        obs_values.reshape(1, -1),
    )
    return resampled, weights.reshape(1, 1, members)


def solution(mesh):
    return jax.shard_map(
        functools.partial(shards, mesh.shape["mem"]),
        mesh=mesh,
        in_specs=(
            P("mem", None, "gx", "gy"),
            P("mem", "gx", "gy"),
            P("gx", "gy", None),
            P("gx", "gy", None),
            P("gx", "gy", None),
        ),
        out_specs=(P("mem", None, "gx", "gy"), P("gx", "gy", "mem")),
        check_vma=False,
    )
```

```python
import functools

import jax
import jax.numpy as jnp
from jax import lax
from jax.experimental import pallas as pl
from jax.experimental.pallas import tpu as pltpu
from jax.sharding import PartitionSpec as P

COURANT = 0.3
NOISE_AMP = 0.1
MESH = pl.DeviceIdType.MESH
BASE = 16
EDGE = 8
STRIPE = 32
CHUNK = 16
LEAD = 3
EARLY = {(0, 1): 0, (1, 0): 2, (1, 1): 3}


def roll_y(a, shift):
    return pltpu.roll(a, shift % a.shape[-1], 1)


def advance(get, force, coriolis):
    def parts(comp):
        mid, low, high = get(comp, 0), get(comp, -1), get(comp, 1)
        near = low + high
        far = get(comp, -2) + get(comp, 2)
        left, right = roll_y(mid, 1), roll_y(mid, -1)
        cross = 0.09 * mid - 0.01 * near
        smooth = (
            0.7 * mid
            + 0.09 * near
            - 0.005 * far
            + roll_y(cross - 0.005 * right, -1)
            + roll_y(cross - 0.005 * left, 1)
        )
        return mid, low, high, left, right, smooth

    _, eta_lo, eta_hi, eta_le, eta_ri, eta_s = parts(0)
    u, u_lo, u_hi, u_le, u_ri, u_s = parts(1)
    v, v_lo, v_hi, v_le, v_ri, v_s = parts(2)
    flux = (
        (1.0 + eta_hi) * u_hi
        - (1.0 + eta_lo) * u_lo
        + (1.0 + eta_ri) * v_ri
        - (1.0 + eta_le) * v_le
    )
    half = 0.5 * COURANT
    new_eta = eta_s - half * flux + NOISE_AMP * force
    turn = COURANT * coriolis
    new_u = u_s - half * (u * (u_hi - u_lo) + v * (u_ri - u_le) + (eta_hi - eta_lo)) + turn * v
    new_v = v_s - half * (u * (v_hi - v_lo) + v * (v_ri - v_le) + (eta_ri - eta_le)) - turn * u
    return new_eta, new_u, new_v


def kernel(
    cfg,
    fields_ref,
    noise_ref,
    anc_ref,
    cells_ref,
    values_ref,
    out_ref,
    weights_ref,
    old,
    mid,
    force,
    seam_own,
    seam_old,
    seam_mid,
    seam_new,
    pack_out,
    pack_in,
    logw_out,
    logw_all,
    *rest,
):
    n, inner, outer, members, count_x, count_y = cfg
    pairs = members // 2
    parts = 12
    strip = count_x // 2
    gathered = rest[0:parts]
    offered = rest[parts : 2 * parts]
    taken = rest[2 * parts : 3 * parts]
    end_out = rest[3 * parts : 4 * parts]
    end_in = rest[4 * parts : 5 * parts]
    (rim_send, rim_recv, w_send, w_recv, z_send, z_recv) = rest[5 * parts : 5 * parts + 6]
    (x_send, x_recv, end_send, end_recv) = rest[5 * parts + 6 :]

    mem, gx, gy = lax.axis_index("mem"), lax.axis_index("gx"), lax.axis_index("gy")
    place, line = lax.rem(mem, inner), lax.div(mem, inner)
    near_x, near_y, diagonal = (mem, 1 - gx, gy), (mem, gx, 1 - gy), (mem, 1 - gx, 1 - gy)

    barrier = pltpu.get_barrier_semaphore()
    for peer in (near_x, near_y, diagonal):
        pl.semaphore_signal(barrier, inc=1, device_id=peer, device_id_type=MESH)
    for d in range(1, n):
        pl.semaphore_signal(
            barrier, inc=1, device_id=(lax.rem(mem + d, n), gx, gy), device_id_type=MESH
        )

    lane = lax.broadcasted_iota(jnp.int32, (1, count_y), 1)
    spot = lane & (STRIPE - 1)
    owner = lane >> 5
    group = spot >> 2
    packed_comp = jnp.where((group & 1) == 1, group >> 1, ((group >> 1) + 1) & 3)

    def seam_of(rows, size, comp):
        total = jnp.zeros((size, count_y), jnp.float32)
        for m in range(members):
            plane = force[m // 2, rows, :] if comp == 3 else old[m, comp, rows, :]
            low = roll_y(plane, 8 + STRIPE * m)
            high = roll_y(plane, 24 + STRIPE * m)
            total = jnp.where(owner == m, jnp.where(spot < 16, low, high), total)
        return total

    def load(i, carry):
        rows = pl.ds(pl.multiple_of(i * CHUNK, CHUNK), CHUNK)
        padded = pl.ds(pl.multiple_of(i * CHUNK + BASE, CHUNK), CHUNK)
        for m in range(members):
            for comp in range(3):
                old[m, comp, padded, :] = fields_ref[m, comp, rows, :]
        for p in range(pairs):
            force[p, padded, :] = noise_ref[p, rows, :]
        packed = jnp.zeros((CHUNK, count_y), jnp.float32)
        for comp in range(4):
            seam = seam_of(padded, CHUNK, comp)
            seam_own[comp, padded, :] = seam
            packed = jnp.where(packed_comp == comp, roll_y(seam, 8 * comp), packed)
        pack_out[rows, :] = packed
        return carry

    lax.fori_loop(0, count_x // CHUNK, load, 0)
    pl.semaphore_wait(barrier, n + 2)

    top = BASE + count_x
    first, last = pl.ds(0, EDGE), pl.ds(count_x - EDGE, EDGE)
    rim_low, rim_high = pl.ds(BASE - EDGE, EDGE), pl.ds(top, EDGE)
    moves = [
        (pack_out, pack_in.at[pl.ds(BASE, count_x), :], near_y),
        (fields_ref.at[:, :, last, :], old.at[:, :, rim_low, :], near_x),
        (fields_ref.at[:, :, first, :], old.at[:, :, rim_high, :], near_x),
        (noise_ref.at[:, last, :], force.at[:, rim_low, :], near_x),
        (noise_ref.at[:, first, :], force.at[:, rim_high, :], near_x),
        (pack_out.at[last, :], pack_in.at[rim_low, :], diagonal),
        (pack_out.at[first, :], pack_in.at[rim_high, :], diagonal),
    ]
    rims = []
    for k, (src, dst, peer) in enumerate(moves):
        rims.append(
            pltpu.make_async_remote_copy(
                src_ref=src,
                dst_ref=dst,
                send_sem=rim_send.at[k],
                recv_sem=rim_recv.at[k],
                device_id=peer,
                device_id_type=MESH,
            )
        )
    for copy in rims:
        copy.start()
    total_y = 2 * count_y

    def turning(local):
        rows_y = lax.rem(gy * count_y + local + total_y, total_y)
        return 0.1 + 0.2 * ((rows_y.astype(jnp.float32) + 0.5) / total_y - 0.5)

    cor_tile = turning(lane)
    cor_seam = turning(jnp.where(spot < 16, spot - 8, spot - 24 + count_y))

    wide = (count_x + 2 * EDGE) // CHUNK

    def first_step(e, low, stride, count):
        def body(i, carry):
            p, k = lax.div(i, count), lax.rem(i, count) * stride + low
            at = pl.multiple_of(k * CHUNK + EDGE, EDGE)
            m = 2 * p + e
            new = advance(
                lambda comp, d: old[m, comp, pl.ds(at + d, CHUNK), :],
                force[p, pl.ds(at, CHUNK), :],
                cor_tile,
            )
            for comp in range(3):
                mid[m, comp, pl.ds(at, CHUNK), :] = new[comp]
            return carry

        lax.fori_loop(0, pairs * count, body, 0, unroll=2)

    first_step(0, 1, 1, wide - 2)
    for copy in rims[1:5]:
        copy.wait_recv()
    first_step(0, 0, wide - 1, 2)

    for start in (BASE - EDGE, top):
        rows = pl.ds(start, EDGE)
        for comp in range(4):
            seam_own[comp, rows, :] = seam_of(rows, EDGE, comp)
    for copy in (rims[0], rims[5], rims[6]):
        copy.wait_recv()

    def seam_fill(i, carry):
        rows = pl.ds(pl.multiple_of(i * CHUNK + EDGE, EDGE), CHUNK)
        packed = pack_in[rows, :]
        for comp in range(4):
            seam_old[comp, rows, :] = jnp.where(
                (spot >= 8) & (spot < 24), seam_own[comp, rows, :], roll_y(packed, -8 * comp)
            )
        return carry

    lax.fori_loop(0, wide, seam_fill, 0)

    def seam_step(source, target):
        def body(i, carry):
            at = pl.multiple_of(i * CHUNK + EDGE, EDGE)
            new = advance(
                lambda comp, d: source[comp, pl.ds(at + d, CHUNK), :],
                seam_old[3, pl.ds(at, CHUNK), :],
                cor_seam,
            )
            for comp in range(3):
                target[comp, pl.ds(at, CHUNK), :] = new[comp]
            return carry

        lax.fori_loop(0, wide, body, 0, unroll=3)

    seam_step(seam_old, seam_mid)
    seam_step(seam_mid, seam_new)

    def z_copy(part, origin, right):
        way = 0 if right else 1
        peer = line + 1 if right else line - 1
        block = gathered[part].at[origin]
        return pltpu.make_async_remote_copy(
            src_ref=block,
            dst_ref=block,
            send_sem=z_send.at[way, part, origin],
            recv_sem=z_recv.at[way, part, origin],
            device_id=(peer * inner + place, gx, gy),
            device_id_type=MESH,
        )

    at_end = (line == 0) | (line == outer - 1)

    def start_own(part, when):
        go_right, go_left = line < outer - 2, line > 1
        if when is not None:
            go_right, go_left = go_right & when, go_left & when

        @pl.when(go_right)
        def _():
            z_copy(part, line, True).start()

        @pl.when(go_left)
        def _():
            z_copy(part, line, False).start()

    def x_copy(part, d):
        return pltpu.make_async_remote_copy(
            src_ref=offered[part].at[d],
            dst_ref=taken[part].at[place],
            send_sem=x_send.at[part, d],
            recv_sem=x_recv.at[part, d],
            device_id=(line * inner + lax.rem(place + d, inner), gx, gy),
            device_id_type=MESH,
        )

    def finish(part):
        e, rows, comp = part // 6, pl.ds(part // 3 % 2 * strip, strip), part % 3
        for d in range(1, inner):
            x_copy(part, d).wait_recv()
        for s in range(pairs):
            source = lax.rem(lax.div(anc_ref[0, mem * pairs + s], pairs), inner)
            out_ref[2 * s + e, comp, rows, :] = taken[part][source, s]

    def end_copy(part):
        end = jnp.where(line == 1, 0, outer - 1)
        return pltpu.make_async_remote_copy(
            src_ref=end_out[part],
            dst_ref=end_in[part],
            send_sem=end_send.at[part],
            recv_sem=end_recv.at[part],
            device_id=(end * inner + place, gx, gy),
            device_id_type=MESH,
        )

    def pick(part, wanted):
        origin = lax.div(lax.div(wanted, pairs), inner)
        return gathered[part][origin, lax.rem(wanted, pairs)]

    def deliver(part):
        @pl.when((line == 1) | (line == outer - 2))
        def _():
            end = jnp.where(line == 1, 0, outer - 1)
            for k in range(inner * pairs):
                end_out[part][k] = pick(part, anc_ref[0, end * inner * pairs + k])
            end_copy(part).start()

        def place_block(d, s, block):
            if d == 0:
                taken[part][place, s] = block
            else:
                offered[part][d, s] = block

        @pl.when(jnp.logical_not(at_end))
        def _():
            for d in range(inner):
                goal = line * inner + lax.rem(place + d, inner)
                for s in range(pairs):
                    place_block(d, s, pick(part, anc_ref[0, goal * pairs + s]))

        @pl.when(at_end)
        def _():
            end_copy(part).wait_recv()
            for d in range(inner):
                spot_in = lax.rem(place + d, inner)
                for s in range(pairs):
                    wanted = anc_ref[0, (line * inner + spot_in) * pairs + s]
                    origin = lax.div(lax.div(wanted, pairs), inner)
                    here = gathered[part][line, 0]
                    for p in range(1, pairs):
                        here = jnp.where(lax.rem(wanted, pairs) == p, gathered[part][line, p], here)
                    sent = end_in[part][spot_in * pairs + s]
                    place_block(d, s, jnp.where(origin == line, here, sent))

        for d in range(1, inner):
            x_copy(part, d).start()

    def w_copy(d):
        return pltpu.make_async_remote_copy(
            src_ref=logw_out,
            dst_ref=logw_all.at[mem],
            send_sem=w_send.at[d],
            recv_sem=w_recv.at[d],
            device_id=(lax.rem(mem + d, n), gx, gy),
            device_id_type=MESH,
        )

    def weigh():
        cells = cells_ref[...]
        hot_y = jnp.where(
            lax.broadcasted_iota(jnp.int32, (count_y, cells.shape[1]), 0) == lax.rem(cells, count_y),
            1.0,
            0.0,
        )
        hot_x = lax.broadcasted_iota(jnp.int32, (count_x, cells.shape[1]), 0) == lax.div(cells, count_y)
        tile_lane = lax.broadcasted_iota(jnp.int32, (8, 128), 1)
        own = jnp.zeros((8, 128), jnp.float32)
        for m in range(members):
            seen = jnp.zeros(cells.shape, jnp.float32)
            for half in range(2):
                picked = jnp.dot(
                    gathered[6 * (m % 2) + 3 * half][line, m // 2],
                    hot_y,
                    precision=lax.Precision.HIGHEST,
                    preferred_element_type=jnp.float32,
                )
                here = hot_x[half * strip : (half + 1) * strip]
                seen += jnp.sum(jnp.where(here, picked, 0.0), axis=0, keepdims=True)
            misfit = seen - values_ref[...]
            logw = -2.0 * jnp.sum(misfit * misfit, axis=1, keepdims=True)
            own = jnp.where(tile_lane == m, logw, own)
        logw_out[...] = own
        logw_all[mem] = own
        for d in range(1, n):
            w_copy(d).start()

    middle = jnp.logical_not(at_end)
    def take_turn(turn):
        for t in range(1, outer):
            part = turn - (t - 1)
            if not 0 <= part < parts:
                continue

            @pl.when((line - t >= 0) & (line < outer - 1))
            def _(part=part, t=t):
                z_copy(part, line - t, True).wait_recv()

                @pl.when(line < outer - 2)
                def _():
                    z_copy(part, line - t, True).start()

            @pl.when((line + t < outer) & (line > 0))
            def _(part=part, t=t):
                z_copy(part, line + t, False).wait_recv()

                @pl.when(line > 1)
                def _():
                    z_copy(part, line + t, False).start()

            if t == 1 and part + LEAD < parts:
                start_own(part + LEAD, middle)
        if turn == 4:
            weigh()
        part = turn - (outer - 2)
        if part >= 0:
            deliver(part)
            if part > 0:
                finish(part - 1)

    for e in range(2):
        if e == 1:
            first_step(1, 0, 1, wide)
            take_turn(1)
        for half in range(2):

            def second_step(i, carry, e=e, half=half):
                p = lax.div(i, strip // CHUNK)
                m = 2 * p + e
                row = pl.multiple_of(lax.rem(i, strip // CHUNK) * CHUNK, CHUNK)
                at = row + (BASE + half * strip)
                new = advance(
                    lambda comp, d: mid[m, comp, pl.ds(at + d, CHUNK), :],
                    force[p, pl.ds(at, CHUNK), :],
                    cor_tile,
                )
                for comp in range(3):
                    seam = seam_new[comp, pl.ds(at, CHUNK), :]
                    low, high = jnp.zeros_like(seam), jnp.zeros_like(seam)
                    for q in range(pairs):
                        base = STRIPE * (2 * q + e)
                        low = jnp.where(p == q, roll_y(seam, -(base + 8)), low)
                        high = jnp.where(p == q, roll_y(seam, -(base + 24)), high)
                    whole = jnp.where(lane < 4, low, jnp.where(lane >= count_y - 4, high, new[comp]))
                    gathered[6 * e + 3 * half + comp][line, p, pl.ds(row, CHUNK), :] = whole
                return carry

            lax.fori_loop(0, pairs * (strip // CHUNK), second_step, 0, unroll=2)
            for comp in range(3):
                part = 6 * e + 3 * half + comp
                start_own(part, None if part < LEAD else at_end)
            if (e, half) in EARLY:
                take_turn(EARLY[e, half])

    for turn in range(4, parts + outer - 2):
        take_turn(turn)
    finish(parts - 1)

    for d in range(1, n):
        w_copy(d).wait_recv()
    every = logw_all[...]
    real = lax.broadcasted_iota(jnp.int32, every.shape, 2) < members
    once = lax.broadcasted_iota(jnp.int32, every.shape, 1) == 0
    every_max = jnp.max(jnp.where(real, every, -jnp.inf), axis=0)
    peak = jnp.max(every_max, axis=1, keepdims=True)
    expo = jnp.where(real & once, jnp.exp(jnp.where(real, every - peak[None], 0.0)), 0.0)
    total = jnp.sum(jnp.sum(jnp.sum(expo, axis=0), axis=1, keepdims=True), axis=0, keepdims=True)
    normal = logw_out[...] - peak - jnp.log(total)
    weights_ref[...] = normal[0:1, 0:members]

    for copy in rims:
        copy.wait_send()
    for d in range(1, n):
        w_copy(d).wait_send()
    for part in range(parts):
        for d in range(1, inner):
            x_copy(part, d).wait_send()

        @pl.when((line == 1) | (line == outer - 2))
        def _(part=part):
            end_copy(part).wait_send()

        for t in range(outer):

            @pl.when((line - t >= 0) & (line < outer - 2))
            def _(part=part, t=t):
                z_copy(part, line - t, True).wait_send()

            @pl.when((line + t < outer) & (line > 1))
            def _(part=part, t=t):
                z_copy(part, line + t, False).wait_send()


def shards(n, fields, noise, ancestors, obs_cells, obs_values):
    members, comps, count_x, count_y = fields.shape
    inner = 1
    while inner * inner * 4 <= n:
        inner *= 2
    outer = n // inner
    pairs = members // 2
    rows = count_x + 2 * BASE
    f32 = jnp.float32
    vmem = pl.BlockSpec(memory_space=pltpu.VMEM)
    dma = pltpu.SemaphoreType.DMA
    parts = 4 * comps
    plane = (count_x // 2, count_y)
    scratch = [
        pltpu.VMEM((members, 3, rows, count_y), f32),
        pltpu.VMEM((members, 3, rows, count_y), f32),
        pltpu.VMEM((pairs, rows, count_y), f32),
        pltpu.VMEM((4, rows, count_y), f32),
        pltpu.VMEM((4, rows, count_y), f32),
        pltpu.VMEM((3, rows, count_y), f32),
        pltpu.VMEM((3, rows, count_y), f32),
        pltpu.VMEM((count_x, count_y), f32),
        pltpu.VMEM((rows, count_y), f32),
        pltpu.VMEM((8, 128), f32),
        pltpu.VMEM((n, 8, 128), f32),
    ]
    scratch += [pltpu.VMEM((outer, pairs) + plane, f32)] * parts
    scratch += [pltpu.VMEM((inner, pairs) + plane, f32)] * (2 * parts)
    scratch += [pltpu.VMEM((inner * pairs,) + plane, f32)] * (2 * parts)
    scratch += [
        dma((7,)),
        dma((7,)),
        dma((n,)),
        dma((n,)),
        dma((2, parts, outer)),
        dma((2, parts, outer)),
        dma((parts, inner)),
        dma((parts, inner)),
        dma((parts,)),
        dma((parts,)),
    ]
    resampled, weights = pl.pallas_call(
        functools.partial(kernel, (n, inner, outer, members, count_x, count_y)),
        out_shape=(
            jax.ShapeDtypeStruct(fields.shape, f32),
            jax.ShapeDtypeStruct((1, members), f32),
        ),
        in_specs=[vmem, vmem, pl.BlockSpec(memory_space=pltpu.SMEM), vmem, vmem],
        out_specs=(vmem, vmem),
        scratch_shapes=scratch,
        compiler_params=pltpu.CompilerParams(
            collective_id=0, has_side_effects=True, vmem_limit_bytes=48 * 1024 * 1024
        ),
    )(
        fields,
        noise,
        ancestors.reshape(1, -1),
        obs_cells.reshape(1, -1),
        obs_values.reshape(1, -1),
    )
    return resampled, weights.reshape(1, 1, members)


def solution(mesh):
    return jax.shard_map(
        functools.partial(shards, mesh.shape["mem"]),
        mesh=mesh,
        in_specs=(
            P("mem", None, "gx", "gy"),
            P("mem", "gx", "gy"),
            P("gx", "gy", None),
            P("gx", "gy", None),
            P("gx", "gy", None),
        ),
        out_specs=(P("mem", None, "gx", "gy"), P("gx", "gy", "mem")),
        check_vma=False,
    )
```

```python
import functools

import jax
import jax.numpy as jnp
from jax import lax
from jax.experimental import pallas as pl
from jax.experimental.pallas import tpu as pltpu
from jax.sharding import PartitionSpec as P

COURANT = 0.3
NOISE_AMP = 0.1
MESH = pl.DeviceIdType.MESH
BASE = 16
EDGE = 8
STRIPE = 32
CHUNK = 16
LEAD = 3
EARLY = {(0, 1): 0, (1, 0): 2, (1, 1): 3}


def roll_y(a, shift):
    return pltpu.roll(a, shift % a.shape[-1], 1)


def advance(get, force, coriolis):
    def parts(comp):
        mid, low, high = get(comp, 0), get(comp, -1), get(comp, 1)
        near = low + high
        far = get(comp, -2) + get(comp, 2)
        left, right = roll_y(mid, 1), roll_y(mid, -1)
        cross = 0.09 * mid - 0.01 * near
        smooth = (
            0.7 * mid
            + 0.09 * near
            - 0.005 * far
            + roll_y(cross - 0.005 * right, -1)
            + roll_y(cross - 0.005 * left, 1)
        )
        return mid, low, high, left, right, smooth

    _, eta_lo, eta_hi, eta_le, eta_ri, eta_s = parts(0)
    u, u_lo, u_hi, u_le, u_ri, u_s = parts(1)
    v, v_lo, v_hi, v_le, v_ri, v_s = parts(2)
    flux = (
        (1.0 + eta_hi) * u_hi
        - (1.0 + eta_lo) * u_lo
        + (1.0 + eta_ri) * v_ri
        - (1.0 + eta_le) * v_le
    )
    half = 0.5 * COURANT
    new_eta = eta_s - half * flux + NOISE_AMP * force
    turn = COURANT * coriolis
    new_u = u_s - half * (u * (u_hi - u_lo) + v * (u_ri - u_le) + (eta_hi - eta_lo)) + turn * v
    new_v = v_s - half * (u * (v_hi - v_lo) + v * (v_ri - v_le) + (eta_ri - eta_le)) - turn * u
    return new_eta, new_u, new_v


def kernel(
    cfg,
    fields_ref,
    noise_ref,
    anc_ref,
    cells_ref,
    values_ref,
    out_ref,
    weights_ref,
    old,
    mid,
    force,
    seam_own,
    seam_old,
    seam_mid,
    seam_new,
    pack_out,
    pack_in,
    logw_out,
    logw_all,
    *rest,
):
    n, inner, outer, members, count_x, count_y = cfg
    pairs = members // 2
    parts = 12
    strip = count_x // 2
    gathered = rest[0:parts]
    offered = rest[parts : 2 * parts]
    taken = rest[2 * parts : 3 * parts]
    end_out = rest[3 * parts : 4 * parts]
    end_in = rest[4 * parts : 5 * parts]
    (rim_send, rim_recv, w_send, w_recv, z_send, z_recv) = rest[5 * parts : 5 * parts + 6]
    (x_send, x_recv, end_send, end_recv) = rest[5 * parts + 6 :]

    mem, gx, gy = lax.axis_index("mem"), lax.axis_index("gx"), lax.axis_index("gy")
    place, line = lax.rem(mem, inner), lax.div(mem, inner)
    near_x, near_y, diagonal = (mem, 1 - gx, gy), (mem, gx, 1 - gy), (mem, 1 - gx, 1 - gy)

    barrier = pltpu.get_barrier_semaphore()
    for peer in (near_x, near_y, diagonal):
        pl.semaphore_signal(barrier, inc=1, device_id=peer, device_id_type=MESH)
    for d in range(1, n):
        pl.semaphore_signal(
            barrier, inc=1, device_id=(lax.rem(mem + d, n), gx, gy), device_id_type=MESH
        )

    lane = lax.broadcasted_iota(jnp.int32, (1, count_y), 1)
    spot = lane & (STRIPE - 1)
    owner = lane >> 5
    group = spot >> 2
    packed_comp = jnp.where((group & 1) == 1, group >> 1, ((group >> 1) + 1) & 3)

    def seam_of(rows, size, comp):
        total = jnp.zeros((size, count_y), jnp.float32)
        for m in range(members):
            plane = force[m // 2, rows, :] if comp == 3 else old[m, comp, rows, :]
            low = roll_y(plane, 8 + STRIPE * m)
            high = roll_y(plane, 24 + STRIPE * m)
            total = jnp.where(owner == m, jnp.where(spot < 16, low, high), total)
        return total

    def load(i, carry):
        rows = pl.ds(pl.multiple_of(i * CHUNK, CHUNK), CHUNK)
        padded = pl.ds(pl.multiple_of(i * CHUNK + BASE, CHUNK), CHUNK)
        for m in range(members):
            for comp in range(3):
                old[m, comp, padded, :] = fields_ref[m, comp, rows, :]
        for p in range(pairs):
            force[p, padded, :] = noise_ref[p, rows, :]
        packed = jnp.zeros((CHUNK, count_y), jnp.float32)
        for comp in range(4):
            seam = seam_of(padded, CHUNK, comp)
            seam_own[comp, padded, :] = seam
            packed = jnp.where(packed_comp == comp, roll_y(seam, 8 * comp), packed)
        pack_out[rows, :] = packed
        return carry

    lax.fori_loop(0, count_x // CHUNK, load, 0)
    pl.semaphore_wait(barrier, n + 2)

    top = BASE + count_x
    first, last = pl.ds(0, EDGE), pl.ds(count_x - EDGE, EDGE)
    rim_low, rim_high = pl.ds(BASE - EDGE, EDGE), pl.ds(top, EDGE)
    moves = [
        (pack_out, pack_in.at[pl.ds(BASE, count_x), :], near_y),
        (fields_ref.at[:, :, last, :], old.at[:, :, rim_low, :], near_x),
        (fields_ref.at[:, :, first, :], old.at[:, :, rim_high, :], near_x),
        (noise_ref.at[:, last, :], force.at[:, rim_low, :], near_x),
        (noise_ref.at[:, first, :], force.at[:, rim_high, :], near_x),
        (pack_out.at[last, :], pack_in.at[rim_low, :], diagonal),
        (pack_out.at[first, :], pack_in.at[rim_high, :], diagonal),
    ]
    rims = []
    for k, (src, dst, peer) in enumerate(moves):
        rims.append(
            pltpu.make_async_remote_copy(
                src_ref=src,
                dst_ref=dst,
                send_sem=rim_send.at[k],
                recv_sem=rim_recv.at[k],
                device_id=peer,
                device_id_type=MESH,
            )
        )
    for copy in rims:
        copy.start()
    total_y = 2 * count_y

    def turning(local):
        rows_y = lax.rem(gy * count_y + local + total_y, total_y)
        return 0.1 + 0.2 * ((rows_y.astype(jnp.float32) + 0.5) / total_y - 0.5)

    cor_tile = turning(lane)
    cor_seam = turning(jnp.where(spot < 16, spot - 8, spot - 24 + count_y))

    wide = (count_x + 2 * EDGE) // CHUNK

    def first_step(e, low, stride, count):
        def body(i, carry):
            p, k = lax.div(i, count), lax.rem(i, count) * stride + low
            at = pl.multiple_of(k * CHUNK + EDGE, EDGE)
            m = 2 * p + e
            new = advance(
                lambda comp, d: old[m, comp, pl.ds(at + d, CHUNK), :],
                force[p, pl.ds(at, CHUNK), :],
                cor_tile,
            )
            for comp in range(3):
                mid[m, comp, pl.ds(at, CHUNK), :] = new[comp]
            return carry

        lax.fori_loop(0, pairs * count, body, 0, unroll=2)

    first_step(0, 1, 1, wide - 2)
    for copy in rims[1:5]:
        copy.wait_recv()
    first_step(0, 0, wide - 1, 2)

    for start in (BASE - EDGE, top):
        rows = pl.ds(start, EDGE)
        for comp in range(4):
            seam_own[comp, rows, :] = seam_of(rows, EDGE, comp)
    for copy in (rims[0], rims[5], rims[6]):
        copy.wait_recv()

    def seam_fill(i, carry):
        rows = pl.ds(pl.multiple_of(i * CHUNK + EDGE, EDGE), CHUNK)
        packed = pack_in[rows, :]
        for comp in range(4):
            seam_old[comp, rows, :] = jnp.where(
                (spot >= 8) & (spot < 24), seam_own[comp, rows, :], roll_y(packed, -8 * comp)
            )
        return carry

    lax.fori_loop(0, wide, seam_fill, 0)

    def seam_step(source, target):
        def body(i, carry):
            at = pl.multiple_of(i * CHUNK + EDGE, EDGE)
            new = advance(
                lambda comp, d: source[comp, pl.ds(at + d, CHUNK), :],
                seam_old[3, pl.ds(at, CHUNK), :],
                cor_seam,
            )
            for comp in range(3):
                target[comp, pl.ds(at, CHUNK), :] = new[comp]
            return carry

        lax.fori_loop(0, wide, body, 0, unroll=3)

    seam_step(seam_old, seam_mid)
    seam_step(seam_mid, seam_new)

    def z_copy(part, origin, right):
        way = 0 if right else 1
        peer = line + 1 if right else line - 1
        block = gathered[part].at[origin]
        return pltpu.make_async_remote_copy(
            src_ref=block,
            dst_ref=block,
            send_sem=z_send.at[way, part, origin],
            recv_sem=z_recv.at[way, part, origin],
            device_id=(peer * inner + place, gx, gy),
            device_id_type=MESH,
        )

    at_end = (line == 0) | (line == outer - 1)

    def start_own(part, when):
        go_right, go_left = line < outer - 2, line > 1
        if when is not None:
            go_right, go_left = go_right & when, go_left & when

        @pl.when(go_right)
        def _():
            z_copy(part, line, True).start()

        @pl.when(go_left)
        def _():
            z_copy(part, line, False).start()

    def x_copy(part, d):
        return pltpu.make_async_remote_copy(
            src_ref=offered[part].at[d],
            dst_ref=taken[part].at[place],
            send_sem=x_send.at[part, d],
            recv_sem=x_recv.at[part, d],
            device_id=(line * inner + lax.rem(place + d, inner), gx, gy),
            device_id_type=MESH,
        )

    def finish(part):
        e, rows, comp = part // 6, pl.ds(part // 3 % 2 * strip, strip), part % 3
        for d in range(1, inner):
            x_copy(part, d).wait_recv()
        for s in range(pairs):
            source = lax.rem(lax.div(anc_ref[0, mem * pairs + s], pairs), inner)
            out_ref[2 * s + e, comp, rows, :] = taken[part][source, s]

    def end_copy(part):
        end = jnp.where(line == 1, 0, outer - 1)
        return pltpu.make_async_remote_copy(
            src_ref=end_out[part],
            dst_ref=end_in[part],
            send_sem=end_send.at[part],
            recv_sem=end_recv.at[part],
            device_id=(end * inner + place, gx, gy),
            device_id_type=MESH,
        )

    def pick(part, wanted):
        origin = lax.div(lax.div(wanted, pairs), inner)
        return gathered[part][origin, lax.rem(wanted, pairs)]

    def deliver(part):
        @pl.when((line == 1) | (line == outer - 2))
        def _():
            end = jnp.where(line == 1, 0, outer - 1)
            for k in range(inner * pairs):
                end_out[part][k] = pick(part, anc_ref[0, end * inner * pairs + k])
            end_copy(part).start()

        def place_block(d, s, block):
            if d == 0:
                taken[part][place, s] = block
            else:
                offered[part][d, s] = block

        @pl.when(jnp.logical_not(at_end))
        def _():
            for d in range(inner):
                goal = line * inner + lax.rem(place + d, inner)
                for s in range(pairs):
                    place_block(d, s, pick(part, anc_ref[0, goal * pairs + s]))

        @pl.when(at_end)
        def _():
            end_copy(part).wait_recv()
            for d in range(inner):
                spot_in = lax.rem(place + d, inner)
                for s in range(pairs):
                    wanted = anc_ref[0, (line * inner + spot_in) * pairs + s]
                    origin = lax.div(lax.div(wanted, pairs), inner)
                    here = gathered[part][line, 0]
                    for p in range(1, pairs):
                        here = jnp.where(lax.rem(wanted, pairs) == p, gathered[part][line, p], here)
                    sent = end_in[part][spot_in * pairs + s]
                    place_block(d, s, jnp.where(origin == line, here, sent))

        for d in range(1, inner):
            x_copy(part, d).start()

    def w_copy(d):
        return pltpu.make_async_remote_copy(
            src_ref=logw_out,
            dst_ref=logw_all.at[mem],
            send_sem=w_send.at[d],
            recv_sem=w_recv.at[d],
            device_id=(lax.rem(mem + d, n), gx, gy),
            device_id_type=MESH,
        )

    def weigh():
        cells = cells_ref[...]
        hot_y = jnp.where(
            lax.broadcasted_iota(jnp.int32, (count_y, cells.shape[1]), 0) == lax.rem(cells, count_y),
            1.0,
            0.0,
        )
        hot_x = lax.broadcasted_iota(jnp.int32, (count_x, cells.shape[1]), 0) == lax.div(cells, count_y)
        tile_lane = lax.broadcasted_iota(jnp.int32, (8, 128), 1)
        own = jnp.zeros((8, 128), jnp.float32)
        for m in range(members):
            seen = jnp.zeros(cells.shape, jnp.float32)
            for half in range(2):
                picked = jnp.dot(
                    gathered[6 * (m % 2) + 3 * half][line, m // 2],
                    hot_y,
                    precision=lax.Precision.HIGHEST,
                    preferred_element_type=jnp.float32,
                )
                here = hot_x[half * strip : (half + 1) * strip]
                seen += jnp.sum(jnp.where(here, picked, 0.0), axis=0, keepdims=True)
            misfit = seen - values_ref[...]
            logw = -2.0 * jnp.sum(misfit * misfit, axis=1, keepdims=True)
            own = jnp.where(tile_lane == m, logw, own)
        logw_out[...] = own
        logw_all[mem] = own
        for d in range(1, n):
            w_copy(d).start()

    middle = jnp.logical_not(at_end)

    def take_turn(turn):
        for t in range(1, outer):
            part = turn - (t - 1)
            if not 0 <= part < parts:
                continue

            @pl.when((line - t >= 0) & (line < outer - 1))
            def _(part=part, t=t):
                z_copy(part, line - t, True).wait_recv()

                @pl.when(line < outer - 2)
                def _():
                    z_copy(part, line - t, True).start()

            @pl.when((line + t < outer) & (line > 0))
            def _(part=part, t=t):
                z_copy(part, line + t, False).wait_recv()

                @pl.when(line > 1)
                def _():
                    z_copy(part, line + t, False).start()

            if t == 1 and part + LEAD < parts:
                start_own(part + LEAD, middle)
        if turn == 4:
            pl.when(at_end)(weigh)
        part = turn - (outer - 2)
        if part >= 0:
            deliver(part)
            if part > 0:
                finish(part - 1)

    for e in range(2):
        if e == 1:
            first_step(1, 0, 1, wide)
            take_turn(1)
        for half in range(2):

            def second_step(i, carry, p, e=e, half=half):
                m = 2 * p + e
                row = pl.multiple_of(i * CHUNK, CHUNK)
                at = row + (BASE + half * strip)
                new = advance(
                    lambda comp, d: mid[m, comp, pl.ds(at + d, CHUNK), :],
                    force[p, pl.ds(at, CHUNK), :],
                    cor_tile,
                )
                for comp in range(3):
                    seam = seam_new[comp, pl.ds(at, CHUNK), :]
                    low, high = roll_y(seam, -(STRIPE * m + 8)), roll_y(seam, -(STRIPE * m + 24))
                    whole = jnp.where(lane < 4, low, jnp.where(lane >= count_y - 4, high, new[comp]))
                    gathered[6 * e + 3 * half + comp][line, p, pl.ds(row, CHUNK), :] = whole
                return carry

            for p in range(pairs):
                body = functools.partial(second_step, p=p)
                lax.fori_loop(0, strip // CHUNK, body, 0, unroll=2)
            for comp in range(3):
                part = 6 * e + 3 * half + comp
                start_own(part, None if part < LEAD else at_end)
            if (e, half) in EARLY:
                take_turn(EARLY[e, half])

    for turn in range(4, parts + outer - 2):
        take_turn(turn)
    pl.when(middle)(weigh)
    finish(parts - 1)

    for d in range(1, n):
        w_copy(d).wait_recv()
    every = logw_all[...]
    real = lax.broadcasted_iota(jnp.int32, every.shape, 2) < members
    once = lax.broadcasted_iota(jnp.int32, every.shape, 1) == 0
    every_max = jnp.max(jnp.where(real, every, -jnp.inf), axis=0)
    peak = jnp.max(every_max, axis=1, keepdims=True)
    expo = jnp.where(real & once, jnp.exp(jnp.where(real, every - peak[None], 0.0)), 0.0)
    total = jnp.sum(jnp.sum(jnp.sum(expo, axis=0), axis=1, keepdims=True), axis=0, keepdims=True)
    normal = logw_out[...] - peak - jnp.log(total)
    weights_ref[...] = normal[0:1, 0:members]

    for copy in rims:
        copy.wait_send()
    for d in range(1, n):
        w_copy(d).wait_send()
    for part in range(parts):
        for d in range(1, inner):
            x_copy(part, d).wait_send()

        @pl.when((line == 1) | (line == outer - 2))
        def _(part=part):
            end_copy(part).wait_send()

        for t in range(outer):

            @pl.when((line - t >= 0) & (line < outer - 2))
            def _(part=part, t=t):
                z_copy(part, line - t, True).wait_send()

            @pl.when((line + t < outer) & (line > 1))
            def _(part=part, t=t):
                z_copy(part, line + t, False).wait_send()


def shards(n, fields, noise, ancestors, obs_cells, obs_values):
    members, comps, count_x, count_y = fields.shape
    inner = 1
    while inner * inner * 4 <= n:
        inner *= 2
    outer = n // inner
    pairs = members // 2
    rows = count_x + 2 * BASE
    f32 = jnp.float32
    vmem = pl.BlockSpec(memory_space=pltpu.VMEM)
    dma = pltpu.SemaphoreType.DMA
    parts = 4 * comps
    plane = (count_x // 2, count_y)
    scratch = [
        pltpu.VMEM((members, 3, rows, count_y), f32),
        pltpu.VMEM((members, 3, rows, count_y), f32),
        pltpu.VMEM((pairs, rows, count_y), f32),
        pltpu.VMEM((4, rows, count_y), f32),
        pltpu.VMEM((4, rows, count_y), f32),
        pltpu.VMEM((3, rows, count_y), f32),
        pltpu.VMEM((3, rows, count_y), f32),
        pltpu.VMEM((count_x, count_y), f32),
        pltpu.VMEM((rows, count_y), f32),
        pltpu.VMEM((8, 128), f32),
        pltpu.VMEM((n, 8, 128), f32),
    ]
    scratch += [pltpu.VMEM((outer, pairs) + plane, f32)] * parts
    scratch += [pltpu.VMEM((inner, pairs) + plane, f32)] * (2 * parts)
    scratch += [pltpu.VMEM((inner * pairs,) + plane, f32)] * (2 * parts)
    scratch += [
        dma((7,)),
        dma((7,)),
        dma((n,)),
        dma((n,)),
        dma((2, parts, outer)),
        dma((2, parts, outer)),
        dma((parts, inner)),
        dma((parts, inner)),
        dma((parts,)),
        dma((parts,)),
    ]
    resampled, weights = pl.pallas_call(
        functools.partial(kernel, (n, inner, outer, members, count_x, count_y)),
        out_shape=(
            jax.ShapeDtypeStruct(fields.shape, f32),
            jax.ShapeDtypeStruct((1, members), f32),
        ),
        in_specs=[vmem, vmem, pl.BlockSpec(memory_space=pltpu.SMEM), vmem, vmem],
        out_specs=(vmem, vmem),
        scratch_shapes=scratch,
        compiler_params=pltpu.CompilerParams(
            collective_id=0, has_side_effects=True, vmem_limit_bytes=48 * 1024 * 1024
        ),
    )(
        fields,
        noise,
        ancestors.reshape(1, -1),
        obs_cells.reshape(1, -1),
        obs_values.reshape(1, -1),
    )
    return resampled, weights.reshape(1, 1, members)


def solution(mesh):
    return jax.shard_map(
        functools.partial(shards, mesh.shape["mem"]),
        mesh=mesh,
        in_specs=(
            P("mem", None, "gx", "gy"),
            P("mem", "gx", "gy"),
            P("gx", "gy", None),
            P("gx", "gy", None),
            P("gx", "gy", None),
        ),
        out_specs=(P("mem", None, "gx", "gy"), P("gx", "gy", "mem")),
        check_vma=False,
    )
```
